32 devices in a mesh: dp: 2 (over core), seq: 16 (over z, y, x).
Axes of the slice: x: 2, y: 2, z: 4, core: 2. Of those that a mesh axis runs over, the one named last changes fastest.
Arguments:
- joints_x: bfloat16 [2, 256, 16, 1536], P('dp', 'seq'), may hold values from -6 to 6
- cotangent: bfloat16 [2, 256, 16, 1536], P('dp', 'seq'), may hold values from -6 to 6
- hidden: int32 [2, 256, 16], P('dp', 'seq'), may hold values 0 or 1
- stream_clip: int32 [2, 256], P('dp'), may hold values from 0 to 271, as said below
- stream_kind: int32 [2, 256], P('dp'), may hold values from 0 to 3, as said below
- adjacency: int32 [4, 136, 136], replicated, may hold values 0 or 1
- mask_token: bfloat16 [1536], replicated, may hold values from -6 to 6
- norm_gain: float32 [1536], replicated, may hold values from 0.1 to 1.9
- w_qkv: bfloat16 [1536, 2304], replicated, may hold values from -0.15625 to 0.15625
- w_out: bfloat16 [768, 1536], replicated, may hold values from -0.21875 to 0.21875
- graph_coef: float32 [12], replicated, may hold values from 0.5 to 260
Outputs:
- layer_out: bfloat16 [2, 256, 16, 1536], P('dp', 'seq')
- grad_x: bfloat16 [2, 256, 16, 1536], P('dp', 'seq')
- grad_token: float32 [1536], replicated
- grad_gain: float32 [1536], replicated
- grad_coef: float32 [12], replicated
The draws below stay inside these ranges and needn't reach their ends.
Inputs may be any that keep to these rules, and one draw needn't show every extreme that they name: `stream_clip`: the slots of a clip are consecutive, clip numbers rise in slot order, starting at 0, at most 16 of them; every slot after the last clip, the last slot always among them, is padding numbered 16 plus its slot index. `stream_kind`: constant within a clip; a clip of kind 0, 1, 2, 3 has 17, 25, 52, 133 slots; slot 0 starts a clip of kind 3; padding slots have kind 0.
All inputs are finite; a program needn't handle non-finite values. No bound on the sum of `hidden` on one device may be relied on, other than what follows from the above.
Results may differ from the reference program's by a relative error of at most 0.0089.
Values may be sent and summed in bfloat16 or wider, within the bound.
No kernel may reach another device: no remote copies, remote signals or barrier semaphores. Data moves between devices by JAX's collectives and lax.ppermute only.
A program may use at most 128 MiB of HBM per device.

```python
import jax
import jax.numpy as jnp
from jax import lax

D = 1536
HEADS = 12
HW = 768
JS = 256
L = 16
NB = 2
KINDS = 4
JMAX = 136


def stream_tables(key):

    def per_batch(batch_idx):
        batch_key = jax.random.fold_in(jax.random.fold_in(key, 101), batch_idx)
        kind_draw = jax.random.randint(batch_key, (16,), 0, 4).astype(jnp.int32).at[0].set(3)
        clip_sizes = jnp.array([17, 25, 52, 133], jnp.int32)[kind_draw]

        def pack_step(position, clip_size):
            clip_fits = position + clip_size <= JS - 1
            clip_start = jnp.where(clip_fits, position, JS)
            clip_stop = jnp.where(clip_fits, position + clip_size, JS)
            return (jnp.where(clip_fits, position + clip_size, position), (clip_start, clip_stop))
        _, (starts, stops) = lax.scan(pack_step, jnp.int32(0), clip_sizes)
        slot_ids = jnp.arange(JS, dtype=jnp.int32)
        in_clip = (slot_ids[:, None] >= starts[None, :]) & (slot_ids[:, None] < stops[None, :])
        is_placed = jnp.any(in_clip, axis=1)
        numbers = jnp.arange(16, dtype=jnp.int32)
        clip_ids = jnp.where(is_placed, jnp.sum(in_clip.astype(jnp.int32) * numbers[None, :], axis=1), 16 + slot_ids)
        kind_ids = jnp.where(is_placed, jnp.sum(in_clip.astype(jnp.int32) * kind_draw[None, :], axis=1), 0)
        return (clip_ids.astype(jnp.int32), kind_ids.astype(jnp.int32))
    return jax.vmap(per_batch)(jnp.arange(NB, dtype=jnp.int32))


def draw_stream_clip(key, part):
    return stream_tables(key)[0]


def draw_stream_kind(key, part):
    return stream_tables(key)[1]


def draw_graph_coef(key, part):
    base_values = jax.random.uniform(jax.random.fold_in(key, 3), (HEADS,), jnp.float32, 0.5, 3.0)
    return base_values


def set_ends(entries, key, smallest, top_value):
    shape = entries.shape
    place = [jax.random.randint(jax.random.fold_in(key, axis), (), 0, shape[axis]) for axis in range(len(shape))]
    entries = entries.at[tuple(place)].set(smallest)
    longest = shape.index(max(shape))
    place[longest] = (place[longest] + 1) % shape[longest]
    return entries.at[tuple(place)].set(top_value)


def shard_levels(key, shape, split, smallest, top_value):
    factor_of = 1.0
    for dim, blocks in split:
        steps = jax.random.uniform(jax.random.fold_in(jax.random.fold_in(key, 6), dim), (blocks,), jnp.float32, smallest / len(split), top_value / len(split))
        factor_of = factor_of * jnp.repeat(jnp.exp(steps), shape[dim] // blocks).reshape((-1,) + (1,) * (len(shape) - 1 - dim))
    return factor_of


def scatter_about(rng, dims, deviation, most, pieces=(), kind=jnp.bfloat16):
    result = deviation * jax.random.normal(rng, dims, jnp.float32)
    if pieces:
        result = result * shard_levels(rng, dims, pieces, -0.22, 0.18)
    return jnp.clip(result, -most, most).astype(kind)


def setup_inputs(seed: int = 0) -> dict:
    keys = jax.random.split(jax.random.key(seed), 12)
    return {
        "joints_x": scatter_about(keys[0], (NB, JS, L, D), 1.0, 6.0, ((0, 2), (1, 16))),
        "cotangent": scatter_about(keys[1], (NB, JS, L, D), 1.0, 6.0, ((0, 2), (1, 16))),
        "hidden": set_ends((jax.random.randint(keys[2], (NB, JS, L), 0, 10) < 3).astype(jnp.int32), jax.random.fold_in(keys[2], 1), 0, 1),
        "stream_clip": draw_stream_clip(jax.random.fold_in(keys[11], 71), 0),
        "stream_kind": draw_stream_kind(jax.random.fold_in(keys[11], 71), 0),
        "adjacency": set_ends((jax.random.randint(keys[5], (KINDS, JMAX, JMAX), 0, 6) < 1).astype(jnp.int32), jax.random.fold_in(keys[5], 1), 0, 1),
        "mask_token": scatter_about(keys[6], (D,), 1.0, 6.0),
        "norm_gain": jnp.clip(1.0 + 0.18 * jax.random.normal(keys[7], (D,), jnp.float32), 0.1, 1.9),
        "w_qkv": scatter_about(keys[8], (D, 3 * HW), D ** -0.5, 0.15625),
        "w_out": scatter_about(keys[9], (HW, D), HW ** -0.5, 0.21875),
        "graph_coef": draw_graph_coef(jax.random.fold_in(keys[11], 71), 0),
    }


def product(form, left, right):
    return jnp.einsum(form, left.astype(jnp.float32), right.astype(jnp.float32))

def frame_tables(clip_ids, kind_ids, adjacency):
    slot_count = clip_ids.shape[0]
    kind_count, joint_max = (adjacency.shape[0], adjacency.shape[1])
    slot_ids = jnp.arange(slot_count, dtype=jnp.int32)
    same_clip = clip_ids[:, None] == clip_ids[None, :]
    first_slot = lax.optimization_barrier(jnp.min(jnp.where(same_clip, slot_ids[None, :], slot_count), axis=1)).astype(jnp.int32)
    joint_idx = slot_ids - first_slot
    table_row = kind_ids * joint_max + joint_idx
    row_pick = (table_row[:, None] == jnp.arange(kind_count * joint_max, dtype=jnp.int32)[None, :]).astype(jnp.float32)
    adj_table = adjacency.reshape(kind_count * joint_max, joint_max).astype(jnp.float32)
    picked = jnp.dot(row_pick, adj_table, precision=lax.Precision.HIGHEST, preferred_element_type=jnp.float32)
    col_pick = (joint_idx[:, None] == jnp.arange(joint_max, dtype=jnp.int32)[None, :]).astype(jnp.float32)
    graph_link = jnp.dot(picked, col_pick.T, precision=lax.Precision.HIGHEST, preferred_element_type=jnp.float32)
    return (same_clip, graph_link)

def attend(x_normed, same_clip, graph_link, graph_coef, w_qkv, w_out):
    slot_count, frame_count = (x_normed.shape[0], x_normed.shape[1])
    head_count = graph_coef.shape[0]
    head_width = w_out.shape[0]
    head_size = head_width // head_count
    score_scale = head_size ** (-0.5)
    united = product('jfd,de->jfe', x_normed, w_qkv).astype(jnp.bfloat16)
    query_part = united[..., :head_width].reshape(slot_count, frame_count, head_count, head_size)
    key_part = united[..., head_width:2 * head_width].reshape(slot_count, frame_count, head_count, head_size)
    value_part = united[..., 2 * head_width:].reshape(slot_count, frame_count, head_count, head_size)
    scores = product('ifhc,jfhc->fhij', query_part, key_part) * score_scale
    scores = scores + graph_coef[None, :, None, None] * graph_link[None, None]
    scores = jnp.where(same_clip[None, None], scores, -jnp.inf)
    row_top = lax.optimization_barrier(jnp.max(scores, axis=-1, keepdims=True))
    shifted = jnp.exp(scores - row_top)
    weights_f = shifted / lax.optimization_barrier(jnp.sum(shifted, axis=-1, keepdims=True))
    weights_b = weights_f.astype(jnp.bfloat16)
    context = product('fhij,jfhc->ifhc', weights_b, value_part).astype(jnp.bfloat16)
    context = context.reshape(slot_count, frame_count, head_width)
    attn_out = product('jfe,ed->jfd', context, w_out).astype(jnp.bfloat16)
    return (attn_out, (query_part, key_part, value_part, weights_f, weights_b))

def attend_back(cot_rows, saved, graph_link, w_qkv, w_out):
    query_part, key_part, value_part, weights_f, weights_b = saved
    slot_count, frame_count, head_count, head_size = query_part.shape
    head_width = head_count * head_size
    score_scale = head_size ** (-0.5)
    grad_context = product('jfd,ed->jfe', cot_rows, w_out).astype(jnp.bfloat16)
    grad_context = grad_context.reshape(slot_count, frame_count, head_count, head_size)
    grad_weights = product('ifhc,jfhc->fhij', grad_context, value_part)
    row_total = lax.optimization_barrier(jnp.sum(weights_f * grad_weights, axis=-1, keepdims=True))
    grad_scores = weights_f * (grad_weights - row_total)
    coef_term = lax.optimization_barrier(jnp.sum(grad_scores * graph_link[None, None], axis=(0, 2, 3)))
    scaled_b = (grad_scores * score_scale).astype(jnp.bfloat16)
    grad_query = product('fhij,jfhc->ifhc', scaled_b, key_part).reshape(slot_count, frame_count, head_width)
    grad_key = product('fhij,ifhc->jfhc', scaled_b, query_part).reshape(slot_count, frame_count, head_width)
    grad_value = product('fhij,ifhc->jfhc', weights_b, grad_context).reshape(slot_count, frame_count, head_width)
    grad_united = jnp.concatenate([grad_query, grad_key, grad_value], axis=-1).astype(jnp.bfloat16)
    grad_normed = product('jfe,de->jfd', grad_united, w_qkv).astype(jnp.bfloat16)
    return (grad_normed, coef_term)

def normalize(x_rows, hidden_on, mask_token, norm_gain):
    x_in = jnp.where(hidden_on, mask_token, x_rows)
    x_float = x_in.astype(jnp.float32)
    root_mean = jnp.sqrt(lax.optimization_barrier(jnp.mean(x_float * x_float, axis=-1, keepdims=True)) + 1e-06)
    x_unit = x_float / root_mean
    x_normed = (x_unit * norm_gain).astype(jnp.bfloat16)
    return (x_float, root_mean, x_unit, x_normed)

def finish(x_float, root_mean, x_unit, hidden_on, attn_back, grad_normed, cot_rows, norm_gain):
    layer_out = (x_float + attn_back.astype(jnp.float32)).astype(jnp.bfloat16)
    gain_grad = grad_normed.astype(jnp.float32) * norm_gain
    grad_input = cot_rows.astype(jnp.float32) + (gain_grad - x_unit * lax.optimization_barrier(jnp.mean(gain_grad * x_unit, axis=-1, keepdims=True))) / root_mean
    grad_x = jnp.where(hidden_on, jnp.float32(0.0), grad_input).astype(jnp.bfloat16)
    lead_axes = tuple(range(grad_input.ndim - 1))
    token_term = lax.optimization_barrier(jnp.sum(jnp.where(hidden_on, grad_input, jnp.float32(0.0)), axis=lead_axes))
    gain_term = lax.optimization_barrier(jnp.sum(grad_normed.astype(jnp.float32) * x_unit, axis=lead_axes))
    return (layer_out, grad_x, token_term, gain_term)

def reference(joints_x, cotangent, hidden, stream_clip, stream_kind, adjacency, mask_token, norm_gain, w_qkv, w_out, graph_coef):
    hidden_on = (hidden == 1)[..., None]
    x_float, root_mean, x_unit, x_normed = normalize(joints_x, hidden_on, mask_token, norm_gain)
    attn_parts = []
    grad_parts = []
    coef_total = jnp.zeros((graph_coef.shape[0],), jnp.float32)
    for batch_idx in range(joints_x.shape[0]):
        same_clip, graph_link = frame_tables(stream_clip[batch_idx], stream_kind[batch_idx], adjacency)
        frames_x = jnp.swapaxes(x_normed[batch_idx], 0, 1)[:, :, None, :]
        frames_cot = jnp.swapaxes(cotangent[batch_idx], 0, 1)[:, :, None, :]

        def per_frame(pair_item, same_clip=same_clip, graph_link=graph_link):
            attn_out, saved = attend(pair_item[0], same_clip, graph_link, graph_coef, w_qkv, w_out)
            grad_normed, coef_term = attend_back(pair_item[1], saved, graph_link, w_qkv, w_out)
            return (attn_out, grad_normed, coef_term)
        outs_attn, outs_grad, coef_terms = lax.map(per_frame, (frames_x, frames_cot))
        attn_parts.append(jnp.swapaxes(outs_attn[:, :, 0, :], 0, 1))
        grad_parts.append(jnp.swapaxes(outs_grad[:, :, 0, :], 0, 1))
        coef_total = coef_total + lax.optimization_barrier(jnp.sum(coef_terms, axis=0))
    attn_back = jnp.stack(attn_parts)
    grad_normed = jnp.stack(grad_parts)
    layer_out, grad_x, token_term, gain_term = finish(x_float, root_mean, x_unit, hidden_on, attn_back, grad_normed, cotangent, norm_gain)
    return (layer_out, grad_x, token_term, gain_term, coef_total)
```

```python
import functools

import jax
import jax.numpy as jnp
import numpy as np
from jax import lax
from jax.experimental import pallas as pl
from jax.experimental.pallas import tpu as pltpu
from jax.sharding import PartitionSpec as P

BF = jnp.bfloat16
F32 = jnp.float32
BIG_CLIP = 133
HIDDEN_MARK = 64.0
MASKED = -1e30
EP = 16
EQ = 8


def dot_nn(a, b):
    return lax.dot_general(a, b, (((1,), (0,)), ((), ())), preferred_element_type=F32)


def dot_nt(a, b):
    return lax.dot_general(a, b, (((1,), (1,)), ((), ())), preferred_element_type=F32)


def dot_tn(a, b):
    return lax.dot_general(a, b, (((0,), (0,)), ((), ())), preferred_element_type=F32)


def iota(shape, axis):
    return lax.broadcasted_iota(jnp.int32, shape, axis)


def hidden_column(hid, slots, frames, frame_major):
    rows = slots * frames
    r = iota((rows, 1), 0)
    slot_of = r % slots if frame_major else r // frames
    frame_of = r // slots if frame_major else r % frames
    pick_slot = (slot_of == iota((rows, slots), 1)).astype(BF)
    by_slot = dot_nn(pick_slot, hid.astype(F32).astype(BF))
    return jnp.sum(jnp.where(frame_of == iota((rows, frames), 1), by_slot, 0.0), axis=1, keepdims=True)


def row_swap(slots, frames, to_frame_major):
    rows = slots * frames
    r = iota((rows, 1), 0)
    if to_frame_major:
        source = (r % slots) * frames + r // slots
    else:
        source = (r % frames) * slots + r // frames
    return (iota((rows, rows), 1) == source).astype(BF)


def send_kernel(slots, frames, x_ref, cot_ref, hid_ref, w_out_ref, out_ref, token_ref):
    width = x_ref.shape[1]
    swap = row_swap(slots, frames, True)
    gc = dot_nt(cot_ref[...], w_out_ref[...]).astype(BF)
    out_ref[:, width:] = dot_nn(swap, gc).astype(BF)
    hid_t = hidden_column(hid_ref[...], slots, frames, True)
    moved = dot_nn(swap, x_ref[...])
    first = jnp.where(
        (iota((moved.shape[0], 128), 1) == 0) & (hid_t > 0.5), HIDDEN_MARK, moved[:, :128]
    )
    out_ref[:, :128] = first.astype(BF)
    out_ref[:, 128:width] = moved[:, 128:].astype(BF)
    hid_s = hidden_column(hid_ref[...], slots, frames, False)
    token_ref[...] = jnp.sum(
        jnp.where(hid_s > 0.5, cot_ref[...].astype(F32), 0.0), axis=0, keepdims=True
    )


def final_kernel(
    slots, frames, recv_ref, x_ref, cot_ref, hid_ref, tok_ref, w_out_ref, out_ref, grad_ref
):
    hw = w_out_ref.shape[0]
    swap = row_swap(slots, frames, False)
    ctx = dot_nn(swap, recv_ref[:, :hw]).astype(BF)
    attn = dot_nn(ctx, w_out_ref[...]).astype(BF)
    hid = hidden_column(hid_ref[...], slots, frames, False) > 0.5
    x_in = jnp.where(hid, tok_ref[...].astype(F32), x_ref[...].astype(F32))
    out_ref[...] = (x_in + attn.astype(F32)).astype(BF)
    delta = dot_nn(swap, recv_ref[:, hw:])
    grad_ref[...] = jnp.where(hid, 0.0, cot_ref[...].astype(F32) + delta).astype(BF)


def frame_kernel(
    blocks,
    nf,
    sb,
    guests,
    recv_ref,
    ext_ref,
    link_ref,
    link_e_ref,
    coef_ref,
    coef_e_ref,
    flag_ref,
    tok_ref,
    gain_ref,
    token_in_ref,
    w_hbm,
    out_ref,
    ext_out_ref,
    sums_ref,
    w_ref,
    xn_s,
    q_s,
    k_s,
    v_s,
    g_s,
    gq_s,
    gk_s,
    gv_s,
    ctx_s,
    sem,
):
    d = gain_ref.shape[1]
    hw = w_ref.shape[1] // 3
    main = blocks * sb
    keys = main + EP
    rows = nf * main
    all_rows = rows + nf * EP
    heads = coef_ref.shape[0]
    hs = hw // heads
    seg_rows = nf * guests

    copies = []
    for c in range(3):
        cp = pltpu.make_async_copy(
            w_hbm.at[:, pl.ds(c * hw, hw)], w_ref.at[:, pl.ds(c * hw, hw)], sem.at[c]
        )
        cp.start()
        copies.append(cp)

    def gather(value):
        if sb % 16 == 0:
            return jnp.concatenate(
                [
                    value[(j * nf + f) * sb : (j * nf + f + 1) * sb]
                    for f in range(nf)
                    for j in range(blocks)
                ],
                axis=0,
            )
        r = iota((rows, 1), 0)
        slot = r % main
        source = ((slot // sb) * nf + r // main) * sb + slot % sb
        return dot_nn((iota((rows, rows), 1) == source).astype(BF), value).astype(BF)

    def scatter(value):
        if sb % 16 == 0:
            return jnp.concatenate(
                [
                    value[f * main + j * sb : f * main + (j + 1) * sb]
                    for j in range(blocks)
                    for f in range(nf)
                ],
                axis=0,
            )
        r = iota((rows, 1), 0)
        pair = r // sb
        source = (pair % nf) * main + (pair // nf) * sb + r % sb
        return dot_nn((iota((rows, rows), 1) == source).astype(BF), value).astype(BF)

    er = iota((nf * EP, 1), 0)
    guest_row = jnp.where(er % EP < guests, (er // EP) * guests + er % EP, 1 << 20)

    def guest_segment(seg):
        pick = (iota((nf * EP, ext_ref.shape[0]), 1) == guest_row + seg * seg_rows).astype(BF)
        return dot_nn(pick, ext_ref[...]).astype(BF)

    x_all = jnp.concatenate(
        [
            gather(recv_ref[:, :d]),
            jnp.concatenate([guest_segment(s) for s in range(d // hw)], axis=1),
        ],
        axis=0,
    ).astype(F32)
    hid = x_all[:, 0:1] > 0.5 * HIDDEN_MARK
    x_all = jnp.where(hid, tok_ref[...].astype(F32), x_all)
    inv = 1.0 / jnp.sqrt(jnp.mean(x_all * x_all, axis=1, keepdims=True) + 1e-6)
    x_unit = x_all * inv
    xn_s[...] = (x_unit * gain_ref[...]).astype(BF)

    gc_main = gather(recv_ref[:, d:])
    gc_ext = guest_segment(d // hw)
    for f in range(nf):
        g_s[f, :main] = gc_main[f * main : (f + 1) * main]
        g_s[f, main:] = gc_ext[f * EP : (f + 1) * EP]

    for c, ref in enumerate((q_s, k_s, v_s)):
        copies[c].wait()
        part = dot_nn(xn_s[...], w_ref[:, c * hw : (c + 1) * hw]).astype(BF)
        if c == 0:
            part = part * BF(hs**-0.5)
        for f in range(nf):
            ref[f, :main] = part[f * main : (f + 1) * main]
            ref[f, main:] = part[rows + f * EP : rows + (f + 1) * EP]

    own = (iota((heads * EQ, hw), 0) // EQ == iota((heads * EQ, hw), 1) // hs)
    link_e = link_e_ref[...]
    bias_e = jnp.where(link_e < 0, MASKED, coef_e_ref[...] * link_e)
    coef_lanes = jnp.zeros((1, heads * EQ), F32)

    def spread(value):
        tall = jnp.concatenate([value] * heads, axis=0)
        return jnp.where(own, tall, jnp.zeros_like(tall))

    def fold(value):
        kept = jnp.where(own, value, 0.0)
        total = kept[0:EQ]
        for h in range(1, heads):
            total = total + kept[h * EQ : (h + 1) * EQ]
        return jnp.concatenate([total, jnp.zeros((EP - EQ, hw), F32)], axis=0)

    for f in range(nf):
        q_e = spread(q_s[f, main:].astype(F32)[:EQ]).astype(BF)
        g_e = spread(g_s[f, main:].astype(F32)[:EQ]).astype(BF)
        s_t = dot_nt(k_s[f], q_e) + bias_e
        p_t = jnp.exp(s_t - jnp.max(s_t, axis=0, keepdims=True))
        w_t = p_t * (1.0 / jnp.sum(p_t, axis=0, keepdims=True))
        w_b = w_t.astype(BF)
        gw = dot_nt(v_s[f], g_e)
        ds = w_t * (gw - jnp.sum(w_t * gw, axis=0, keepdims=True))
        coef_lanes = coef_lanes + jnp.sum(ds * link_e, axis=0, keepdims=True)
        ds_b = ds.astype(BF)
        ctx_s[f, main:] = fold(dot_tn(w_b, v_s[f])).astype(BF)
        gq_s[f, main:] = fold(dot_tn(ds_b, k_s[f]) * hs**-0.5).astype(BF)
        gk_s[f] = dot_nn(ds_b, q_e)
        gv_s[f] = dot_nn(w_b, g_e)

    lane = iota((1, 128), 1)
    coef_out = jnp.zeros((1, 128), F32)
    for h in range(heads):
        coef_out = coef_out + jnp.where(
            lane == h, jnp.sum(coef_lanes[:, h * EQ : (h + 1) * EQ]), 0.0
        )

    pair_w = 2 * hs
    low = iota((main, pair_w), 1) < hs
    zero = jnp.zeros((main, pair_w), BF)
    link = link_ref[...]
    for p in range(heads // 2):
        cols = slice(p * pair_w, (p + 1) * pair_w)
        bias = jnp.concatenate(
            [
                jnp.where(link < 0, MASKED, coef_ref[2 * p] * link),
                jnp.where(link < 0, MASKED, coef_ref[2 * p + 1] * link),
            ],
            axis=1,
        )
        ds_sum = jnp.zeros((keys, 2 * main), F32)
        for f in range(nf):
            k = k_s[f, :, cols]
            v = v_s[f, :, cols]
            q = q_s[f, :main, cols]
            g = g_s[f, :main, cols]
            qq = jnp.concatenate([jnp.where(low, q, zero), jnp.where(low, zero, q)], axis=0)
            gg = jnp.concatenate([jnp.where(low, g, zero), jnp.where(low, zero, g)], axis=0)
            s_t = dot_nt(k, qq) + bias
            p_t = jnp.exp(s_t - jnp.max(s_t, axis=0, keepdims=True))
            w_t = p_t * (1.0 / jnp.sum(p_t, axis=0, keepdims=True))
            w_b = w_t.astype(BF)
            gw = dot_nt(v, gg)
            ds = w_t * (gw - jnp.sum(w_t * gw, axis=0, keepdims=True))
            ds_sum = ds_sum + ds
            ds_b = ds.astype(BF)
            ctx_t = dot_tn(v, w_b)
            ctx_t = jnp.concatenate([ctx_t[:hs, :main], ctx_t[hs:, main:]], axis=0)
            ctx_s[f, :main, cols] = ctx_t.T.astype(BF)
            gq_t = dot_tn(k, ds_b)
            gq_t = jnp.concatenate([gq_t[:hs, :main], gq_t[hs:, main:]], axis=0)
            gq_s[f, :main, cols] = (gq_t.T * hs**-0.5).astype(BF)
            gk_s[f, :, cols] += dot_nn(ds_b, qq)
            gv_s[f, :, cols] += dot_nn(w_b, gg)
        lanes = jnp.sum(ds_sum * jnp.concatenate([link, link], axis=1), axis=0, keepdims=True)
        coef_out = coef_out + jnp.where(lane == 2 * p, jnp.sum(lanes[:, :main]), 0.0)
        coef_out = coef_out + jnp.where(lane == 2 * p + 1, jnp.sum(lanes[:, main:]), 0.0)

    def stacked(ref):
        return jnp.concatenate(
            [ref[f, :main].astype(BF) for f in range(nf)]
            + [ref[f, main:].astype(BF) for f in range(nf)],
            axis=0,
        )

    gn = dot_nt(stacked(gq_s), w_ref[:, :hw])
    gn = gn + dot_nt(stacked(gk_s), w_ref[:, hw : 2 * hw])
    gn = gn + dot_nt(stacked(gv_s), w_ref[:, 2 * hw :])
    first_half = flag_ref[0] == 1
    r = iota((all_rows, 1), 0)
    is_guest = r >= rows
    place = jnp.where(is_guest, (r - rows) % EP, r % main)
    guest_limit = jnp.where(first_half, guests, 0)
    main_limit = jnp.where(first_half, 0, guests)
    valid = (is_guest & (place < guest_limit)) | (~is_guest & (place >= main_limit))
    gx = gn * x_unit
    g_gain = gn * gain_ref[...]
    mean_gx = jnp.mean(g_gain * x_unit, axis=1, keepdims=True)
    delta = (g_gain - x_unit * mean_gx) * inv
    sums_ref[:, :d] = token_in_ref[...] + jnp.sum(
        jnp.where(valid & hid, delta, 0.0), axis=0, keepdims=True
    )
    sums_ref[:, d : 2 * d] = jnp.sum(jnp.where(valid, gx, 0.0), axis=0, keepdims=True)
    sums_ref[:, 2 * d :] = coef_out
    delta = delta.astype(BF)
    ctx = stacked(ctx_s)
    out_ref[:, :hw] = scatter(ctx[:rows])
    out_ref[:, hw:] = scatter(delta[:rows])

    orow = iota((ext_out_ref.shape[0], 1), 0)
    inner = orow % seg_rows
    ext_total = jnp.zeros(ext_out_ref.shape, F32)
    for s in range(1 + d // hw):
        piece = ctx[rows:] if s == 0 else delta[rows:, (s - 1) * hw : s * hw]
        source = jnp.where(
            orow // seg_rows == s, (inner // guests) * EP + inner % guests, 1 << 20
        )
        ext_total = ext_total + dot_nn(
            (iota((ext_out_ref.shape[0], nf * EP), 1) == source).astype(BF), piece
        )
    ext_out_ref[...] = ext_total.astype(BF)


VMEM = pl.BlockSpec(memory_space=pltpu.VMEM)
SMEM = pl.BlockSpec(memory_space=pltpu.SMEM)
HBM = pl.BlockSpec(memory_space=pl.ANY)


def table_kernel(half_slots, guests, heads, flag_ref, clip_ref, kind_ref, adj_ref, link_ref, link_e_ref, adj_s):
    first_half = flag_ref[0]
    total = clip_ref.shape[1]
    kind_count, joint_max = adj_ref.shape[0], adj_ref.shape[1]
    keys = half_slots + EP
    adj_s[...] = jnp.zeros(adj_s.shape, F32)
    adj_s[:, :joint_max, :joint_max] = adj_ref[...].astype(F32)
    i = iota((keys, 1), 0)
    slot = jnp.where(i < half_slots, i + jnp.where(first_half == 1, 0, half_slots), i)
    valid = ((i < half_slots) & (i >= jnp.where(first_half == 1, 0, guests))) | (
        (i >= half_slots) & (i < jnp.where(first_half == 1, half_slots + guests, 0))
    )
    lanes = iota((keys, total), 1)
    at = lanes == slot
    clip_row = clip_ref[...].astype(F32)
    clip = jnp.sum(jnp.where(at, clip_row, 0.0), axis=1, keepdims=True)
    kind = jnp.sum(jnp.where(at, kind_ref[...].astype(F32), 0.0), axis=1, keepdims=True)
    first = jnp.min(
        jnp.where(clip_row == clip, lanes.astype(F32), 1.0 * total), axis=1, keepdims=True
    )
    joint = slot.astype(F32) - first
    clip = jnp.where(valid, clip, -1.0 - i.astype(F32))
    pick = (iota((keys, adj_s.shape[1]), 1).astype(F32) == joint).astype(BF)
    picked = jnp.zeros((keys, adj_s.shape[2]), F32)
    for k in range(kind_count):
        picked = picked + jnp.where(kind == 1.0 * k, dot_nn(pick, adj_s[k].astype(BF)), 0.0)
    link = dot_nt(pick, picked.astype(BF))
    eye = iota((keys, keys), 0) == iota((keys, keys), 1)
    clip_across = jnp.sum(jnp.where(eye, clip, 0.0), axis=0, keepdims=True)
    link = jnp.where(clip == clip_across, link, -1.0)
    link_ref[...] = link[:, :half_slots]
    tile = (iota((EP, heads * EQ), 1) % EQ == iota((EP, heads * EQ), 0)).astype(BF)
    link_e_ref[...] = dot_nn(link[:, half_slots:].astype(BF), tile)


def on_device(
    n,
    joints_x,
    cotangent,
    hidden,
    stream_clip,
    stream_kind,
    adjacency,
    mask_token,
    norm_gain,
    w_qkv,
    w_out,
    graph_coef,
):
    _, slots, frames, d = joints_x.shape
    hw = w_out.shape[0]
    heads = graph_coef.shape[0]
    total = stream_clip.shape[1]
    half = n // 2
    nf = frames // half
    half_slots = total // 2
    guests = BIG_CLIP - half_slots
    rows = slots * frames
    wide = d + hw
    segs = wide // hw
    me = lax.axis_index("seq")
    first_half = me < half
    groups = [list(range(half)), list(range(half, n))]

    x = joints_x.reshape(rows, d)
    cot = cotangent.reshape(rows, d)
    hid = hidden[0]
    tok = mask_token.reshape(1, d)

    send, token_cot = pl.pallas_call(
        functools.partial(send_kernel, slots, frames),
        out_shape=(
            jax.ShapeDtypeStruct((rows, wide), BF),
            jax.ShapeDtypeStruct((1, d), F32),
        ),
        in_specs=[VMEM] * 4,
        out_specs=(VMEM, VMEM),
        compiler_params=pltpu.CompilerParams(vmem_limit_bytes=40 << 20),
        name="send",
    )(x, cot, hid, w_out)

    recv = lax.all_to_all(send, "seq", 0, 0, axis_index_groups=groups, tiled=True)

    flag = first_half.astype(jnp.int32).reshape(1)
    joint_pad = -(-adjacency.shape[1] // 256) * 256
    link, link_e = pl.pallas_call(
        functools.partial(table_kernel, half_slots, guests, heads),
        out_shape=(
            jax.ShapeDtypeStruct((half_slots + EP, half_slots), F32),
            jax.ShapeDtypeStruct((half_slots + EP, heads * EQ), F32),
        ),
        in_specs=[SMEM, VMEM, VMEM, VMEM],
        out_specs=(VMEM, VMEM),
        scratch_shapes=[pltpu.VMEM((adjacency.shape[0], joint_pad, joint_pad), F32)],
        compiler_params=pltpu.CompilerParams(vmem_limit_bytes=24 << 20),
        cost_estimate=pl.CostEstimate(flops=400_000_000, bytes_accessed=600_000, transcendentals=0),
        name="tables",
    )(flag, stream_clip, stream_kind, adjacency)

    def buffer_row(f, e):
        return ((e // slots) * nf + f) * slots + e % slots

    run = min(slots, guests)
    starts = [
        (buffer_row(f, e), min(run, guests - e)) for f in range(nf) for e in range(0, guests, run)
    ]
    ext_rows = -(-segs * nf * guests // 16) * 16
    pieces = [
        recv[a : a + c, s * hw : (s + 1) * hw] for s in range(segs) for a, c in starts
    ]
    pieces.append(jnp.zeros((ext_rows - segs * nf * guests, hw), BF))
    ext = lax.ppermute(
        jnp.concatenate(pieces, axis=0), "seq", [(half + i, i) for i in range(half)]
    )

    main = half_slots
    all_rows = rows + nf * EP
    out, ext_out, sums = pl.pallas_call(
        functools.partial(frame_kernel, half, nf, slots, guests),
        out_shape=(
            jax.ShapeDtypeStruct((rows, wide), BF),
            jax.ShapeDtypeStruct((ext_rows, hw), BF),
            jax.ShapeDtypeStruct((1, 2 * d + 128), F32),
        ),
        in_specs=[VMEM, VMEM, VMEM, VMEM, SMEM, VMEM, SMEM, VMEM, VMEM, VMEM, HBM],
        out_specs=(VMEM, VMEM, VMEM),
        scratch_shapes=[
            pltpu.VMEM((d, 3 * hw), BF),
            pltpu.VMEM((all_rows, d), BF),
            pltpu.VMEM((nf, main + EP, hw), BF),
            pltpu.VMEM((nf, main + EP, hw), BF),
            pltpu.VMEM((nf, main + EP, hw), BF),
            pltpu.VMEM((nf, main + EP, hw), BF),
            pltpu.VMEM((nf, main + EP, hw), BF),
            pltpu.VMEM((nf, main + EP, hw), F32),
            pltpu.VMEM((nf, main + EP, hw), F32),
            pltpu.VMEM((nf, main + EP, hw), BF),
            pltpu.SemaphoreType.DMA((3,)),
        ],
        compiler_params=pltpu.CompilerParams(vmem_limit_bytes=56 << 20),
        name="frames",
    )(
        recv,
        ext,
        link,
        link_e,
        graph_coef,
        jnp.repeat(graph_coef, EQ).reshape(1, heads * EQ),
        flag,
        tok,
        norm_gain.reshape(1, d),
        token_cot,
        w_qkv,
    )

    back = lax.ppermute(ext_out, "seq", [(i, half + i) for i in range(half)])
    at = 0
    merged = out
    for a, c in starts:
        new = jnp.concatenate(
            [back[s * nf * guests + at : s * nf * guests + at + c] for s in range(segs)], axis=1
        )
        new = jnp.where(first_half, out[a : a + c], new)
        merged = merged.at[a : a + c].set(new)
        at += c
    returned = lax.all_to_all(merged, "seq", 0, 0, axis_index_groups=groups, tiled=True)

    sums = sums + lax.ppermute(sums, "dp", [(0, 1), (1, 0)])
    k = 1
    while k < n:
        sums = sums + lax.ppermute(sums, "seq", [(i, i ^ k) for i in range(n)])
        k *= 2

    layer_out, grad_x = pl.pallas_call(
        functools.partial(final_kernel, slots, frames),
        out_shape=(
            jax.ShapeDtypeStruct((rows, d), BF),
            jax.ShapeDtypeStruct((rows, d), BF),
        ),
        in_specs=[VMEM] * 6,
        out_specs=(VMEM, VMEM),
        compiler_params=pltpu.CompilerParams(vmem_limit_bytes=48 << 20),
        name="final",
    )(returned, x, cot, hid, tok, w_out)

    shape = (1, slots, frames, d)
    return (
        layer_out.reshape(shape),
        grad_x.reshape(shape),
        sums[0, :d],
        sums[0, d : 2 * d],
        sums[0, 2 * d : 2 * d + heads],
    )


def solution(mesh):
    return jax.shard_map(
        functools.partial(on_device, mesh.shape["seq"]),
        mesh=mesh,
        in_specs=(
            P("dp", "seq", None, None),
            P("dp", "seq", None, None),
            P("dp", "seq", None),
            P("dp", None),
            P("dp", None),
            P(),
            P(),
            P(),
            P(),
            P(),
            P(),
        ),
        out_specs=(P("dp", "seq", None, None), P("dp", "seq", None, None), P(), P(), P()),
        check_vma=False,
    )
```

```python
import functools

import jax
import jax.numpy as jnp
import numpy as np
from jax import lax
from jax.experimental import pallas as pl
from jax.experimental.pallas import tpu as pltpu
from jax.sharding import PartitionSpec as P

BF = jnp.bfloat16
F32 = jnp.float32
BIG_CLIP = 133
HIDDEN_MARK = 64.0
MASKED = -1e30
EP = 16
EQ = 8
VMEM_LIMIT = 16 << 20
FRAMES_LIMIT = 50 << 20
SEND_LIMIT = 56 << 20
SUMS = 5
LANES = 256


def dot_nn(a, b):
    return lax.dot_general(a, b, (((1,), (0,)), ((), ())), preferred_element_type=F32)


def dot_nt(a, b):
    return lax.dot_general(a, b, (((1,), (1,)), ((), ())), preferred_element_type=F32)


def dot_tn(a, b):
    return lax.dot_general(a, b, (((0,), (0,)), ((), ())), preferred_element_type=F32)


def iota(shape, axis):
    return lax.broadcasted_iota(jnp.int32, shape, axis)


def hidden_column(hid, slots, frames, frame_major):
    rows = slots * frames
    r = iota((rows, 1), 0)
    slot_of = r % slots if frame_major else r // frames
    frame_of = r // slots if frame_major else r % frames
    pick_slot = (slot_of == iota((rows, slots), 1)).astype(BF)
    by_slot = dot_nn(pick_slot, hid.astype(F32).astype(BF))
    return jnp.sum(jnp.where(frame_of == iota((rows, frames), 1), by_slot, 0.0), axis=1, keepdims=True)


def row_swap(slots, frames, to_frame_major):
    rows = slots * frames
    r = iota((rows, 1), 0)
    if to_frame_major:
        source = (r % slots) * frames + r // slots
    else:
        source = (r % frames) * slots + r // frames
    return (iota((rows, rows), 1) == source).astype(BF)


def send_kernel(
    slots,
    frames,
    x_hbm,
    cot_hbm,
    hid_hbm,
    w_out_hbm,
    out_ref,
    token_ref,
    x_ref,
    cot_ref,
    hid_ref,
    w_ref,
    sem,
):
    width = x_ref.shape[1]
    copies = [
        pltpu.make_async_copy(hid_hbm, hid_ref, sem.at[0]),
        pltpu.make_async_copy(x_hbm, x_ref, sem.at[1]),
        pltpu.make_async_copy(cot_hbm, cot_ref, sem.at[2]),
        pltpu.make_async_copy(w_out_hbm, w_ref, sem.at[3]),
    ]
    for cp in copies:
        cp.start()
    swap = row_swap(slots, frames, True)
    copies[0].wait()
    hid_t = hidden_column(hid_ref[...], slots, frames, True)
    hid_s = hidden_column(hid_ref[...], slots, frames, False)
    copies[1].wait()
    moved = dot_nn(swap, x_ref[...])
    first = jnp.where(
        (iota((moved.shape[0], 128), 1) == 0) & (hid_t > 0.5), HIDDEN_MARK, moved[:, :128]
    )
    out_ref[:, :128] = first.astype(BF)
    out_ref[:, 128:width] = moved[:, 128:].astype(BF)
    copies[2].wait()
    token_ref[...] = jnp.sum(
        jnp.where(hid_s > 0.5, cot_ref[...].astype(F32), 0.0), axis=0, keepdims=True
    )
    copies[3].wait()
    gc = dot_nt(cot_ref[...], w_ref[...]).astype(BF)
    out_ref[:, width:] = dot_nn(swap, gc).astype(BF)


def final_kernel(
    slots,
    frames,
    shared,
    recv_ref,
    x_hbm,
    cot_hbm,
    hid_ref,
    tok_ref,
    w_ref,
    sums_ref,
    out_hbm,
    grad_hbm,
    token_ref,
    gain_ref,
    coef_ref,
    x_ref,
    cot_ref,
    out_s,
    grad_s,
    sem,
):
    hw, d = w_ref.shape
    wide = hw + d
    copies = [
        pltpu.make_async_copy(cot_hbm, cot_ref, sem.at[0]),
        pltpu.make_async_copy(x_hbm, x_ref, sem.at[1]),
    ]
    for cp in copies:
        cp.start()
    swap = row_swap(slots, frames, False)
    hid = hidden_column(hid_ref[...], slots, frames, False) > 0.5
    delta = dot_nn(swap, recv_ref[:, hw:wide])
    ctx = dot_nn(swap, recv_ref[:, :hw]).astype(BF)
    copies[0].wait()
    grad_s[...] = jnp.where(hid, 0.0, cot_ref[...].astype(F32) + delta).astype(BF)
    stores = [
        pltpu.make_async_copy(grad_s, grad_hbm, sem.at[2]),
        pltpu.make_async_copy(out_s, out_hbm, sem.at[3]),
    ]
    stores[0].start()
    attn = dot_nn(ctx, w_ref[...]).astype(BF)
    copies[1].wait()
    x_in = jnp.where(hid, tok_ref[...].astype(F32), x_ref[...].astype(F32))
    out_s[...] = (x_in + attn.astype(F32)).astype(BF)
    stores[1].start()
    if shared:
        total = jnp.zeros((32, LANES), F32)
        for j in range(recv_ref.shape[0] // 32):
            total = total + recv_ref[j * 32 : (j + 1) * 32, wide:].astype(F32)
        total = total[:16] + total[16:]
        parts = d // LANES
        for c in range(parts):
            here = pl.ds(c * LANES, LANES)
            token_ref[here] = total[c : c + 1].reshape(LANES)
            gain_ref[here] = total[parts + c : parts + c + 1].reshape(LANES)
        coef_ref[...] = total[2 * parts : 2 * parts + 1, : coef_ref.shape[1]]
    else:
        for c in range(d // hw):
            here = pl.ds(c * hw, hw)
            token_ref[here] = sums_ref[c : c + 1].reshape(hw)
            gain_ref[here] = sums_ref[2 + c : 3 + c].reshape(hw)
        coef_ref[...] = sums_ref[4:5, : coef_ref.shape[1]]
    for cp in stores:
        cp.wait()


def split_two(value):
    high = value.astype(BF)
    return high, (value - high.astype(F32)).astype(BF)


def merge_kernel(
    nf, sb, guests, wide, head_rows, flag_ref, buf_ref, own_ref, got_ref, core_ref, cross_ref, out_ref, sums_ref
):
    hw = got_ref.shape[1]
    segs = wide // hw
    seg_rows = nf * guests
    total_rows = out_ref.shape[0]
    i = iota((8, got_ref.shape[0]), 0)
    k = iota((8, got_ref.shape[0]), 1) - segs * seg_rows
    pick = ((i < SUMS) & ((k == i) | (k == i + SUMS))).astype(BF)
    sums = (own_ref[...] + dot_nn(pick, got_ref[...])) + (core_ref[...] + cross_ref[...])
    sums_ref[...] = sums
    if out_ref.shape[1] > wide:
        flat = jnp.concatenate(
            [sums[a : a + 1, c : c + LANES] for a in range(SUMS) for c in range(0, hw, LANES)]
            + [jnp.zeros((1, LANES), F32)],
            axis=0,
        )
        block = jnp.concatenate(split_two(flat), axis=0)
        for j in range(total_rows // block.shape[0]):
            out_ref[j * block.shape[0] : (j + 1) * block.shape[0], wide:] = block
    r = iota((head_rows, 1), 0)
    slot = (r // (nf * sb)) * sb + r % sb
    from_row = ((r // sb) % nf) * guests + slot
    guest = jnp.where(slot < guests, 1, 0)
    take = guest * jnp.where(flag_ref[0] == 1, 0, 1)
    for s in range(segs):
        source = jnp.where(guest == 1, s * seg_rows + from_row, 1 << 20)
        pick = (iota((head_rows, got_ref.shape[0]), 1) == source).astype(BF)
        here = slice(s * hw, (s + 1) * hw)
        out_ref[:head_rows, here] = jnp.where(
            take == 1, dot_nn(pick, got_ref[...]), buf_ref[:head_rows, here].astype(F32)
        ).astype(BF)


def local_tables(half_slots, guests, heads, first_half, clip_ref, kind_ref, adj_ref, adj_s):
    total = clip_ref.shape[1]
    kind_count, joint_max = adj_ref.shape[0], adj_ref.shape[1]
    keys = half_slots + EP
    adj_s[...] = jnp.zeros(adj_s.shape, F32)
    adj_s[:, :joint_max, :joint_max] = adj_ref[...].astype(F32)
    i = iota((keys, 1), 0)
    slot = jnp.where(i < half_slots, i + jnp.where(first_half == 1, 0, half_slots), i)
    valid = ((i < half_slots) & (i >= jnp.where(first_half == 1, 0, guests))) | (
        (i >= half_slots) & (i < jnp.where(first_half == 1, half_slots + guests, 0))
    )
    lanes = iota((keys, total), 1)
    at = lanes == slot
    clip_row = clip_ref[...].astype(F32)
    clip = jnp.sum(jnp.where(at, clip_row, 0.0), axis=1, keepdims=True)
    kind = jnp.sum(jnp.where(at, kind_ref[...].astype(F32), 0.0), axis=1, keepdims=True)
    first = jnp.min(
        jnp.where(clip_row == clip, lanes.astype(F32), 1.0 * total), axis=1, keepdims=True
    )
    joint = slot.astype(F32) - first
    clip = jnp.where(valid, clip, -1.0 - i.astype(F32))
    pick = (iota((keys, adj_s.shape[1]), 1).astype(F32) == joint).astype(BF)
    picked = jnp.zeros((keys, adj_s.shape[2]), F32)
    for k in range(kind_count):
        picked = picked + jnp.where(kind == 1.0 * k, dot_nn(pick, adj_s[k].astype(BF)), 0.0)
    link = dot_nt(pick, picked.astype(BF))
    eye = iota((keys, keys), 0) == iota((keys, keys), 1)
    clip_across = jnp.sum(jnp.where(eye, clip, 0.0), axis=0, keepdims=True)
    link = jnp.where(clip == clip_across, link, -1.0)
    tile = (iota((EP, heads * EQ), 1) % EQ == iota((EP, heads * EQ), 0)).astype(BF)
    return link[:, :half_slots], dot_nn(link[:, half_slots:].astype(BF), tile)


def stage_kernel(
    half_slots, guests, heads, nf, sb, count, flag_ref, send_ref, clip_ref, kind_ref, adj_ref, *refs
):
    link_ref, link_e_ref = refs[:2]
    ext_refs = refs[2 : 2 + count]
    adj_s = refs[-1]

    @pl.when(flag_ref[1] == count)
    def _():
        for j, ref in enumerate(ext_refs):
            ext_rows, hw = ref.shape
            pieces = [
                send_ref[(j * nf + f) * sb : (j * nf + f + 1) * sb, c : c + hw].astype(F32)[:guests]
                for c in range(0, send_ref.shape[1], hw)
                for f in range(nf)
            ]
            pieces.append(jnp.zeros((ext_rows - len(pieces) * guests, hw), F32))
            ref[...] = jnp.concatenate(pieces, axis=0).astype(BF)

    link, link_e = local_tables(
        half_slots, guests, heads, flag_ref[0], clip_ref, kind_ref, adj_ref, adj_s
    )
    link_ref[...] = link
    link_e_ref[...] = link_e


def frame_kernel(
    blocks,
    nf,
    sb,
    guests,
    *refs,
):
    (
        ext_ref,
        recv_ref,
        flag_ref,
        link_ref,
        link_e_ref,
        coef_ref,
        coef_e_ref,
        tok_ref,
        gain_ref,
        token_in_ref,
        w_hbm,
        out_s,
        pay_ref,
        sums_ref,
        x_s,
        xn_s,
        inv_s,
        hid_s,
        q_s,
        k_s,
        v_s,
        g_s,
        gu_s,
        gk_s,
        gv_s,
        ctx_s,
        gn_s,
        w_ref,
        sem,
    ) = refs
    d = gain_ref.shape[1]
    hw = w_ref.shape[1] // 3
    main = blocks * sb
    keys = main + EP
    rows = nf * main
    all_rows = rows + nf * EP
    heads = coef_ref.shape[0]
    hs = hw // heads
    seg_rows = nf * guests
    aligned = sb % 16 == 0

    copies = [pltpu.make_async_copy(w_hbm, w_ref, sem.at[0])]
    for cp in copies:
        cp.start()
    link = link_ref[...]
    link_e = link_e_ref[...]

    def gather(value):
        if aligned:
            return jnp.concatenate(
                [
                    value[(j * nf + f) * sb : (j * nf + f + 1) * sb]
                    for f in range(nf)
                    for j in range(blocks)
                ],
                axis=0,
            )
        r = iota((rows, 1), 0)
        slot = r % main
        source = ((slot // sb) * nf + r // main) * sb + slot % sb
        return dot_nn((iota((rows, rows), 1) == source).astype(BF), value).astype(BF)

    def scatter(value):
        if aligned:
            return jnp.concatenate(
                [
                    value[f * main + j * sb : f * main + (j + 1) * sb]
                    for j in range(blocks)
                    for f in range(nf)
                ],
                axis=0,
            )
        r = iota((rows, 1), 0)
        pair = r // sb
        source = (pair % nf) * main + (pair // nf) * sb + r % sb
        return dot_nn((iota((rows, rows), 1) == source).astype(BF), value).astype(BF)

    er = iota((nf * EP, 1), 0)
    guest_row = jnp.where(er % EP < guests, (er // EP) * guests + er % EP, 1 << 20)

    def guest_segment(seg):
        pick = (iota((nf * EP, ext_ref.shape[0]), 1) == guest_row + seg * seg_rows).astype(BF)
        return dot_nn(pick, ext_ref[...]).astype(BF)

    for c in range(d // hw):
        x_s[rows:, c * hw : (c + 1) * hw] = guest_segment(c)
    x_s[:rows] = gather(recv_ref[:, :d])
    tok = tok_ref[...]
    gain = gain_ref[...]
    for a in range(0, all_rows, 16):
        xb = x_s[a : a + 16]
        hid = xb[:, 0:1].astype(F32) > 0.5 * HIDDEN_MARK
        xf = jnp.where(hid, tok.astype(F32), xb.astype(F32))
        x_s[a : a + 16] = xf.astype(BF)
        inv = 1.0 / jnp.sqrt(jnp.mean(xf * xf, axis=1, keepdims=True) + 1e-6)
        inv_s[a : a + 16] = jnp.broadcast_to(inv, (16, 128))
        hid_s[a : a + 16] = jnp.broadcast_to(jnp.where(hid, 1.0, 0.0), (16, 128))
        xn_s[a : a + 16] = (xf * inv * gain).astype(BF)

    for cp in copies:
        cp.wait()
    for c, ref in enumerate((q_s, k_s, v_s)):
        part = dot_nn(xn_s[...], w_ref[:, c * hw : (c + 1) * hw]).astype(BF)
        if c == 0:
            part = part * BF(hs**-0.5)
        for f in range(nf):
            ref[f, :main] = part[f * main : (f + 1) * main]
            ref[f, main:] = part[rows + f * EP : rows + (f + 1) * EP]

    gc_main = gather(recv_ref[:, d:])
    gc_ext = guest_segment(d // hw)
    for f in range(nf):
        g_s[f, :main] = gc_main[f * main : (f + 1) * main]
        g_s[f, main:] = gc_ext[f * EP : (f + 1) * EP]

    own = (iota((heads * EQ, hw), 0) // EQ == iota((heads * EQ, hw), 1) // hs)
    bias_e = jnp.where(link_e < 0, MASKED, coef_e_ref[...] * link_e)
    coef_lanes = jnp.zeros((1, heads * EQ), F32)

    def spread(value):
        tall = jnp.concatenate([value] * heads, axis=0)
        return jnp.where(own, tall, jnp.zeros_like(tall))

    def fold(value):
        kept = jnp.where(own, value, 0.0)
        total = kept[0:EQ]
        for h in range(1, heads):
            total = total + kept[h * EQ : (h + 1) * EQ]
        return jnp.concatenate([total, jnp.zeros((EP - EQ, hw), F32)], axis=0)

    for f in range(nf):
        guest_rows = slice(rows + f * EP, rows + (f + 1) * EP)
        q_e = spread(q_s[f, main:].astype(F32)[:EQ]).astype(BF)
        g_e = spread(g_s[f, main:].astype(F32)[:EQ]).astype(BF)
        s_t = dot_nt(k_s[f], q_e) + bias_e
        p_t = jnp.exp(s_t - jnp.max(s_t, axis=0, keepdims=True))
        w_t = p_t * (1.0 / jnp.sum(p_t, axis=0, keepdims=True))
        w_b = w_t.astype(BF)
        gw = dot_nt(v_s[f], g_e)
        ds = w_t * (gw - jnp.sum(w_t * gw, axis=0, keepdims=True))
        coef_lanes = coef_lanes + jnp.sum(ds * link_e, axis=0, keepdims=True)
        ds_b = ds.astype(BF)
        ctx_s[guest_rows] = fold(dot_tn(w_b, v_s[f])).astype(BF)
        gu_s[guest_rows, :hw] = fold(dot_tn(ds_b, k_s[f]) * hs**-0.5).astype(BF)
        gk_s[f] = dot_nn(ds_b, q_e)
        gv_s[f] = dot_nn(w_b, g_e)

    lane = iota((1, 128), 1)
    coef_out = jnp.zeros((1, 128), F32)
    for h in range(heads):
        coef_out = coef_out + jnp.where(
            lane == h, jnp.sum(coef_lanes[:, h * EQ : (h + 1) * EQ]), 0.0
        )

    pair_w = 2 * hs
    low = iota((main, pair_w), 1) < hs
    zero = jnp.zeros((main, pair_w), BF)
    for p in range(heads // 2):
        cols = slice(p * pair_w, (p + 1) * pair_w)
        k_cols = slice(hw + p * pair_w, hw + (p + 1) * pair_w)
        v_cols = slice(2 * hw + p * pair_w, 2 * hw + (p + 1) * pair_w)
        bias = jnp.concatenate(
            [
                jnp.where(link < 0, MASKED, coef_ref[2 * p] * link),
                jnp.where(link < 0, MASKED, coef_ref[2 * p + 1] * link),
            ],
            axis=1,
        )
        ds_sum = jnp.zeros((keys, 2 * main), F32)
        for f in range(nf):
            main_rows = slice(f * main, (f + 1) * main)
            guest_rows = slice(rows + f * EP, rows + (f + 1) * EP)
            k = k_s[f, :, cols]
            v = v_s[f, :, cols]
            q = q_s[f, :main, cols]
            g = g_s[f, :main, cols]
            qq = jnp.concatenate([jnp.where(low, q, zero), jnp.where(low, zero, q)], axis=0)
            gg = jnp.concatenate([jnp.where(low, g, zero), jnp.where(low, zero, g)], axis=0)
            s_t = dot_nt(k, qq) + bias
            p_t = jnp.exp(s_t - jnp.max(s_t, axis=0, keepdims=True))
            w_t = p_t * (1.0 / jnp.sum(p_t, axis=0, keepdims=True))
            w_b = w_t.astype(BF)
            gw = dot_nt(v, gg)
            ds = w_t * (gw - jnp.sum(w_t * gw, axis=0, keepdims=True))
            ds_sum = ds_sum + ds
            ds_b = ds.astype(BF)
            ctx_t = dot_tn(v, w_b)
            ctx_t = jnp.concatenate([ctx_t[:hs, :main], ctx_t[hs:, main:]], axis=0)
            ctx_s[main_rows, cols] = ctx_t.T.astype(BF)
            gq_t = dot_tn(k, ds_b)
            gq_t = jnp.concatenate([gq_t[:hs, :main], gq_t[hs:, main:]], axis=0)
            gu_s[main_rows, cols] = (gq_t.T * hs**-0.5).astype(BF)
            gk = (gk_s[f, :, cols] + dot_nn(ds_b, qq)).astype(BF)
            gu_s[main_rows, k_cols] = gk[:main]
            gu_s[guest_rows, k_cols] = gk[main:]
            gv = (gv_s[f, :, cols] + dot_nn(w_b, gg)).astype(BF)
            gu_s[main_rows, v_cols] = gv[:main]
            gu_s[guest_rows, v_cols] = gv[main:]
        lanes = jnp.sum(ds_sum * jnp.concatenate([link, link], axis=1), axis=0, keepdims=True)
        coef_out = coef_out + jnp.where(lane == 2 * p, jnp.sum(lanes[:, :main]), 0.0)
        coef_out = coef_out + jnp.where(lane == 2 * p + 1, jnp.sum(lanes[:, main:]), 0.0)

    out_s[:, :hw] = scatter(ctx_s[:rows])
    gn_s[...] = dot_nt(gu_s[...], w_ref[...])
    guest_limit = jnp.where(flag_ref[0] == 1, guests, 0)
    main_limit = jnp.where(flag_ref[0] == 1, 0, guests)
    place = iota((16, 1), 0)
    token_sum = jnp.zeros((8, d), F32)
    gain_sum = jnp.zeros((8, d), F32)
    for a in range(0, all_rows, 16):
        gn = gn_s[a : a + 16]
        inv = inv_s[a : a + 16, 0:1]
        x_unit = x_s[a : a + 16].astype(F32) * inv
        g_gain = gn * gain
        gx = gn * x_unit
        mean_gx = jnp.mean(gx * gain, axis=1, keepdims=True)
        delta = (g_gain - x_unit * mean_gx) * inv
        if a >= rows:
            x_s[a : a + 16] = delta.astype(BF)
            valid = jnp.where(place < guest_limit, 1.0, 0.0)
        elif aligned:
            f, j = a // main, (a % main) // sb
            at = (j * nf + f) * sb + a % sb
            out_s[at : at + 16, hw : hw + d] = delta.astype(BF)
            valid = jnp.where(place + a % main >= main_limit, 1.0, 0.0)
        else:
            x_s[a : a + 16] = delta.astype(BF)
            valid = jnp.where(place + a % main >= main_limit, 1.0, 0.0)
        hid_valid = hid_s[a : a + 16, 0:1] * valid
        if a >= rows or a % main < guests:
            gx = gx * valid
        delta = delta * hid_valid
        gain_sum = gain_sum + (gx[:8] + gx[8:])
        token_sum = token_sum + (delta[:8] + delta[8:])
    if not aligned:
        out_s[:, hw : hw + d] = scatter(x_s[:rows])
    gain_sum = jnp.sum(gain_sum, axis=0, keepdims=True)
    token_sum = token_in_ref[...] + jnp.sum(token_sum, axis=0, keepdims=True)
    coef_row = jnp.concatenate([coef_out, jnp.zeros((1, hw - coef_out.shape[1]), F32)], axis=1)
    sums = jnp.concatenate(
        [token_sum[:, :hw], token_sum[:, hw:], gain_sum[:, :hw], gain_sum[:, hw:], coef_row]
        + [jnp.zeros((8 - SUMS, hw), F32)],
        axis=0,
    )
    high, low_part = split_two(sums)
    sums_ref[...] = high.astype(F32) + low_part.astype(F32)
    pair = jnp.concatenate([high.astype(F32), low_part.astype(F32)], axis=0).astype(BF)
    orow = iota((pay_ref.shape[0], 1), 0)
    k = orow - (1 + d // hw) * seg_rows
    source = jnp.where(
        k < 0, 1 << 20, jnp.where(k < SUMS, k, jnp.where(k < 2 * SUMS, k - SUMS + 8, 1 << 20))
    )
    total = dot_nn((iota((pay_ref.shape[0], 16), 1) == source).astype(BF), pair)
    inner = orow % seg_rows
    for s in range(1 + d // hw):
        piece = ctx_s[rows:] if s == 0 else x_s[rows:, (s - 1) * hw : s * hw]
        source = jnp.where(
            orow // seg_rows == s, (inner // guests) * EP + inner % guests, 1 << 20
        )
        total = total + dot_nn(
            (iota((pay_ref.shape[0], nf * EP), 1) == source).astype(BF), piece
        )
    pay_ref[...] = total.astype(BF)


VMEM = pl.BlockSpec(memory_space=pltpu.VMEM)
SMEM = pl.BlockSpec(memory_space=pltpu.SMEM)
HBM = pl.BlockSpec(memory_space=pl.ANY)


def on_device(
    n,
    joints_x,
    cotangent,
    hidden,
    stream_clip,
    stream_kind,
    adjacency,
    mask_token,
    norm_gain,
    w_qkv,
    w_out,
    graph_coef,
):
    _, slots, frames, d = joints_x.shape
    hw = w_out.shape[0]
    heads = graph_coef.shape[0]
    total = stream_clip.shape[1]
    half = n // 2
    nf = frames // half
    half_slots = total // 2
    guests = BIG_CLIP - half_slots
    rows = slots * frames
    wide = d + hw
    segs = wide // hw
    me = lax.axis_index("seq")
    first_half = me < half
    groups = [list(range(half)), list(range(half, n))]

    x = joints_x.reshape(rows, d)
    cot = cotangent.reshape(rows, d)
    hid = hidden[0]
    tok = mask_token.reshape(1, d)
    flag = jnp.stack([first_half.astype(jnp.int32), me])

    send, token_cot = pl.pallas_call(
        functools.partial(send_kernel, slots, frames),
        out_shape=(
            jax.ShapeDtypeStruct((rows, wide), BF),
            jax.ShapeDtypeStruct((1, d), F32),
        ),
        in_specs=[HBM] * 4,
        out_specs=(VMEM, VMEM),
        scratch_shapes=[
            pltpu.VMEM((rows, d), BF),
            pltpu.VMEM((rows, d), BF),
            pltpu.VMEM(hid.shape, jnp.int32),
            pltpu.VMEM(w_out.shape, BF),
            pltpu.SemaphoreType.DMA((4,)),
        ],
        compiler_params=pltpu.CompilerParams(vmem_limit_bytes=SEND_LIMIT),
        name="send",
    )(x, cot, hid, w_out)

    recv = lax.all_to_all(send, "seq", 0, 0, axis_index_groups=groups, tiled=True)

    def buffer_row(f, e):
        return ((e // slots) * nf + f) * slots + e % slots

    run = min(slots, guests)
    starts = [
        (buffer_row(f, e), min(run, guests - e)) for f in range(nf) for e in range(0, guests, run)
    ]
    ext_rows = -(-segs * nf * guests // 16) * 16
    direct = slots >= guests and slots % 16 == 0 and half <= 8
    joint_pad = -(-adjacency.shape[1] // 256) * 256
    keys = half_slots + EP
    count = half if direct else 0
    link, link_e, *packed = pl.pallas_call(
        functools.partial(stage_kernel, half_slots, guests, heads, nf, slots, count),
        out_shape=(
            jax.ShapeDtypeStruct((keys, half_slots), F32),
            jax.ShapeDtypeStruct((keys, heads * EQ), F32),
        )
        + (jax.ShapeDtypeStruct((ext_rows, hw), BF),) * count,
        in_specs=[SMEM] + [VMEM] * 4,
        out_specs=(VMEM,) * (2 + count),
        scratch_shapes=[pltpu.VMEM((adjacency.shape[0], joint_pad, joint_pad), F32)],
        compiler_params=pltpu.CompilerParams(vmem_limit_bytes=VMEM_LIMIT),
        name="stage",
    )(flag, send, stream_clip, stream_kind, adjacency)
    if direct:
        ext = lax.ppermute(packed[0], "seq", [(half, 0)])
        for j in range(1, half):
            ext = ext + lax.ppermute(packed[j], "seq", [(half, j)])
    else:
        pieces = [
            recv[a : a + c, s * hw : (s + 1) * hw] for s in range(segs) for a, c in starts
        ]
        pieces.append(jnp.zeros((ext_rows - segs * nf * guests, hw), BF))
        ext = lax.ppermute(
            jnp.concatenate(pieces, axis=0), "seq", [(half + i, i) for i in range(half)]
        )

    main = half_slots
    all_rows = rows + nf * EP
    block_rows = nf * slots
    shared = block_rows % 32 == 0
    out_wide = wide + (LANES if shared else 0)
    head_rows = -(-guests // slots) * block_rows
    head_rows = -(-head_rows // 16) * 16
    pay_rows = -(-(segs * nf * guests + 2 * SUMS) // 8) * 8
    per_frame = (nf, main + EP, hw)
    out, pay, own_sums = pl.pallas_call(
        functools.partial(frame_kernel, half, nf, slots, guests),
        out_shape=(
            jax.ShapeDtypeStruct((rows, out_wide), BF),
            jax.ShapeDtypeStruct((pay_rows, hw), BF),
            jax.ShapeDtypeStruct((8, hw), F32),
        ),
        in_specs=[VMEM, VMEM, SMEM, VMEM, VMEM, SMEM, VMEM, VMEM, VMEM, VMEM, HBM],
        out_specs=(VMEM, VMEM, VMEM),
        scratch_shapes=[
            pltpu.VMEM((all_rows, d), BF),
            pltpu.VMEM((all_rows, d), BF),
            pltpu.VMEM((all_rows, 128), F32),
            pltpu.VMEM((all_rows, 128), F32),
            pltpu.VMEM(per_frame, BF),
            pltpu.VMEM(per_frame, BF),
            pltpu.VMEM(per_frame, BF),
            pltpu.VMEM(per_frame, BF),
            pltpu.VMEM((all_rows, 3 * hw), BF),
            pltpu.VMEM(per_frame, F32),
            pltpu.VMEM(per_frame, F32),
            pltpu.VMEM((all_rows, hw), BF),
            pltpu.VMEM((all_rows, d), F32),
            pltpu.VMEM((d, 3 * hw), BF),
            pltpu.SemaphoreType.DMA((3,)),
        ],
        compiler_params=pltpu.CompilerParams(vmem_limit_bytes=FRAMES_LIMIT),
        name="frames",
    )(
        ext,
        recv,
        flag,
        link,
        link_e,
        graph_coef,
        jnp.repeat(graph_coef, EQ).reshape(1, heads * EQ),
        tok,
        norm_gain.reshape(1, d),
        token_cot,
        w_qkv,
    )

    flip = [(i, (i + half) % n) for i in range(n)]
    got = lax.ppermute(pay, "seq", flip)
    core = lax.ppermute(own_sums, "dp", [(0, 1), (1, 0)])
    cross = lax.ppermute(
        own_sums, ("dp", "seq"), [(c * n + i, (1 - c) * n + j) for c in range(2) for i, j in flip]
    )
    merged, sums = pl.pallas_call(
        functools.partial(merge_kernel, nf, slots, guests, wide, head_rows),
        out_shape=(
            jax.ShapeDtypeStruct((rows, out_wide), BF),
            jax.ShapeDtypeStruct((8, hw), F32),
        ),
        in_specs=[SMEM] + [VMEM] * 5,
        out_specs=(VMEM, VMEM),
        input_output_aliases={1: 0},
        compiler_params=pltpu.CompilerParams(vmem_limit_bytes=VMEM_LIMIT),
        name="merge",
    )(flag, out, own_sums, got, core, cross)
    returned = lax.all_to_all(merged, "seq", 0, 0, axis_index_groups=groups, tiled=True)

    if not shared:
        k = 1
        while k < half:
            sums = sums + lax.ppermute(sums, "seq", [(i, i ^ k) for i in range(n)])
            k *= 2

    layer_out, grad_x, token, gain, coef = pl.pallas_call(
        functools.partial(final_kernel, slots, frames, shared),
        out_shape=(
            jax.ShapeDtypeStruct((rows, d), BF),
            jax.ShapeDtypeStruct((rows, d), BF),
            jax.ShapeDtypeStruct((d,), F32),
            jax.ShapeDtypeStruct((d,), F32),
            jax.ShapeDtypeStruct((1, heads), F32),
        ),
        in_specs=[VMEM, HBM, HBM, VMEM, VMEM, VMEM, VMEM],
        out_specs=(HBM, HBM, VMEM, VMEM, VMEM),
        scratch_shapes=[
            pltpu.VMEM((rows, d), BF),
            pltpu.VMEM((rows, d), BF),
            pltpu.VMEM((rows, d), BF),
            pltpu.VMEM((rows, d), BF),
            pltpu.SemaphoreType.DMA((4,)),
        ],
        compiler_params=pltpu.CompilerParams(vmem_limit_bytes=VMEM_LIMIT),
        name="final",
    )(returned, x, cot, hid, tok, w_out, sums)

    shape = (1, slots, frames, d)
    return (
        layer_out.reshape(shape),
        grad_x.reshape(shape),
        token,
        gain,
        coef.reshape(-1),
    )


def solution(mesh):
    return jax.shard_map(
        functools.partial(on_device, mesh.shape["seq"]),
        mesh=mesh,
        in_specs=(
            P("dp", "seq", None, None),
            P("dp", "seq", None, None),
            P("dp", "seq", None),
            P("dp", None),
            P("dp", None),
            P(),
            P(),
            P(),
            P(),
            P(),
            P(),
        ),
        out_specs=(P("dp", "seq", None, None), P("dp", "seq", None, None), P(), P(), P()),
        check_vma=False,
    )
```

```python
import functools

import jax
import jax.numpy as jnp
import numpy as np
from jax import lax
from jax.experimental import pallas as pl
from jax.experimental.pallas import tpu as pltpu
from jax.sharding import PartitionSpec as P

BF = jnp.bfloat16
F32 = jnp.float32
BIG_CLIP = 133
HIDDEN_MARK = 64.0
MASKED = -1e30
EP = 16
EQ = 8
VMEM_LIMIT = 16 << 20
FRAMES_LIMIT = 50 << 20
SEND_LIMIT = 56 << 20
SUMS = 5
LANES = 256


def dot_nn(a, b):
    return lax.dot_general(a, b, (((1,), (0,)), ((), ())), preferred_element_type=F32)


def dot_nt(a, b):
    return lax.dot_general(a, b, (((1,), (1,)), ((), ())), preferred_element_type=F32)


def dot_tn(a, b):
    return lax.dot_general(a, b, (((0,), (0,)), ((), ())), preferred_element_type=F32)


def iota(shape, axis):
    return lax.broadcasted_iota(jnp.int32, shape, axis)


def hidden_column(hid, slots, frames, frame_major):
    rows = slots * frames
    r = iota((rows, 1), 0)
    slot_of = r % slots if frame_major else r // frames
    frame_of = r // slots if frame_major else r % frames
    pick_slot = (slot_of == iota((rows, slots), 1)).astype(BF)
    by_slot = dot_nn(pick_slot, hid.astype(F32).astype(BF))
    return jnp.sum(jnp.where(frame_of == iota((rows, frames), 1), by_slot, 0.0), axis=1, keepdims=True)


def row_swap(slots, frames, to_frame_major):
    rows = slots * frames
    r = iota((rows, 1), 0)
    if to_frame_major:
        source = (r % slots) * frames + r // slots
    else:
        source = (r % frames) * slots + r // frames
    return (iota((rows, rows), 1) == source).astype(BF)


def send_kernel(
    slots,
    frames,
    x_hbm,
    cot_hbm,
    hid_hbm,
    w_out_hbm,
    out_ref,
    token_ref,
    x_ref,
    cot_ref,
    hid_ref,
    w_ref,
    sem,
):
    width = x_ref.shape[1]
    copies = [
        pltpu.make_async_copy(hid_hbm, hid_ref, sem.at[0]),
        pltpu.make_async_copy(x_hbm, x_ref, sem.at[1]),
        pltpu.make_async_copy(cot_hbm, cot_ref, sem.at[2]),
        pltpu.make_async_copy(w_out_hbm, w_ref, sem.at[3]),
    ]
    for cp in copies:
        cp.start()
    swap = row_swap(slots, frames, True)
    copies[0].wait()
    hid_t = hidden_column(hid_ref[...], slots, frames, True)
    hid_s = hidden_column(hid_ref[...], slots, frames, False)
    copies[1].wait()
    moved = dot_nn(swap, x_ref[...])
    first = jnp.where(
        (iota((moved.shape[0], 128), 1) == 0) & (hid_t > 0.5), HIDDEN_MARK, moved[:, :128]
    )
    out_ref[:, :128] = first.astype(BF)
    out_ref[:, 128:width] = moved[:, 128:].astype(BF)
    copies[2].wait()
    token_ref[...] = jnp.sum(
        jnp.where(hid_s > 0.5, cot_ref[...].astype(F32), 0.0), axis=0, keepdims=True
    )
    copies[3].wait()
    gc = dot_nt(cot_ref[...], w_ref[...]).astype(BF)
    out_ref[:, width:] = dot_nn(swap, gc).astype(BF)


def final_kernel(
    slots,
    frames,
    shared,
    recv_ref,
    x_hbm,
    cot_hbm,
    hid_ref,
    tok_ref,
    w_ref,
    sums_ref,
    out_hbm,
    grad_hbm,
    token_ref,
    gain_ref,
    coef_ref,
    x_ref,
    cot_ref,
    out_s,
    grad_s,
    sem,
):
    hw, d = w_ref.shape
    wide = hw + d
    copies = [
        pltpu.make_async_copy(cot_hbm, cot_ref, sem.at[0]),
        pltpu.make_async_copy(x_hbm, x_ref, sem.at[1]),
    ]
    for cp in copies:
        cp.start()
    swap = row_swap(slots, frames, False)
    hid = hidden_column(hid_ref[...], slots, frames, False) > 0.5
    if shared:
        total = jnp.zeros((32, LANES), F32)
        for j in range(recv_ref.shape[0] // 32):
            total = total + recv_ref[j * 32 : (j + 1) * 32, wide:].astype(F32)
        total = total[:16] + total[16:]
        parts = d // LANES
        for c in range(parts):
            here = pl.ds(c * LANES, LANES)
            token_ref[here] = total[c : c + 1].reshape(LANES)
            gain_ref[here] = total[parts + c : parts + c + 1].reshape(LANES)
        coef_ref[...] = total[2 * parts : 2 * parts + 1, : coef_ref.shape[1]]
    else:
        for c in range(d // hw):
            here = pl.ds(c * hw, hw)
            token_ref[here] = sums_ref[c : c + 1].reshape(hw)
            gain_ref[here] = sums_ref[2 + c : 3 + c].reshape(hw)
        coef_ref[...] = sums_ref[4:5, : coef_ref.shape[1]]
    ctx = dot_nn(swap, recv_ref[:, :hw]).astype(BF)
    attn = dot_nn(ctx, w_ref[...]).astype(BF)
    delta = dot_nn(swap, recv_ref[:, hw:wide])
    for cp in copies:
        cp.wait()
    stores = []
    half = swap.shape[0] // 2
    for h in range(2):
        r = slice(h * half, (h + 1) * half)
        here = pl.ds(h * half, half)
        grad_s[r] = jnp.where(hid[r], 0.0, cot_ref[r].astype(F32) + delta[r]).astype(BF)
        stores.append(pltpu.make_async_copy(grad_s.at[here], grad_hbm.at[here], sem.at[2 + 2 * h]))
        stores[-1].start()
        x_in = jnp.where(hid[r], tok_ref[...].astype(F32), x_ref[r].astype(F32))
        out_s[r] = (x_in + attn[r].astype(F32)).astype(BF)
        stores.append(pltpu.make_async_copy(out_s.at[here], out_hbm.at[here], sem.at[3 + 2 * h]))
        stores[-1].start()
    for cp in stores:
        cp.wait()


def split_two(value):
    high = value.astype(BF)
    return high, (value - high.astype(F32)).astype(BF)


def merge_kernel(
    nf, sb, guests, wide, head_rows, flag_ref, buf_ref, own_ref, got_ref, core_ref, cross_ref, out_ref, sums_ref
):
    hw = got_ref.shape[1]
    segs = wide // hw
    seg_rows = nf * guests
    total_rows = out_ref.shape[0]
    i = iota((8, got_ref.shape[0]), 0)
    k = iota((8, got_ref.shape[0]), 1) - segs * seg_rows
    pick = ((i < SUMS) & ((k == i) | (k == i + SUMS))).astype(BF)
    sums = (own_ref[...] + dot_nn(pick, got_ref[...])) + (core_ref[...] + cross_ref[...])
    sums_ref[...] = sums
    if out_ref.shape[1] > wide:
        flat = jnp.concatenate(
            [sums[a : a + 1, c : c + LANES] for a in range(SUMS) for c in range(0, hw, LANES)]
            + [jnp.zeros((1, LANES), F32)],
            axis=0,
        )
        block = jnp.concatenate(split_two(flat), axis=0)
        for j in range(total_rows // block.shape[0]):
            out_ref[j * block.shape[0] : (j + 1) * block.shape[0], wide:] = block
    r = iota((head_rows, 1), 0)
    slot = (r // (nf * sb)) * sb + r % sb
    from_row = ((r // sb) % nf) * guests + slot
    guest = jnp.where(slot < guests, 1, 0)
    take = guest * jnp.where(flag_ref[0] == 1, 0, 1)
    for s in range(segs):
        source = jnp.where(guest == 1, s * seg_rows + from_row, 1 << 20)
        pick = (iota((head_rows, got_ref.shape[0]), 1) == source).astype(BF)
        here = slice(s * hw, (s + 1) * hw)
        out_ref[:head_rows, here] = jnp.where(
            take == 1, dot_nn(pick, got_ref[...]), buf_ref[:head_rows, here].astype(F32)
        ).astype(BF)


def local_tables(half_slots, guests, heads, first_half, clip_ref, kind_ref, adj_ref, adj_s):
    total = clip_ref.shape[1]
    kind_count, joint_max = adj_ref.shape[0], adj_ref.shape[1]
    keys = half_slots + EP
    adj_s[...] = jnp.zeros(adj_s.shape, F32)
    adj_s[:, :joint_max, :joint_max] = adj_ref[...].astype(F32)
    i = iota((keys, 1), 0)
    slot = jnp.where(i < half_slots, i + jnp.where(first_half == 1, 0, half_slots), i)
    valid = ((i < half_slots) & (i >= jnp.where(first_half == 1, 0, guests))) | (
        (i >= half_slots) & (i < jnp.where(first_half == 1, half_slots + guests, 0))
    )
    lanes = iota((keys, total), 1)
    at = lanes == slot
    clip_row = clip_ref[...].astype(F32)
    clip = jnp.sum(jnp.where(at, clip_row, 0.0), axis=1, keepdims=True)
    kind = jnp.sum(jnp.where(at, kind_ref[...].astype(F32), 0.0), axis=1, keepdims=True)
    first = jnp.min(
        jnp.where(clip_row == clip, lanes.astype(F32), 1.0 * total), axis=1, keepdims=True
    )
    joint = slot.astype(F32) - first
    clip = jnp.where(valid, clip, -1.0 - i.astype(F32))
    pick = (iota((keys, adj_s.shape[1]), 1).astype(F32) == joint).astype(BF)
    picked = jnp.zeros((keys, adj_s.shape[2]), F32)
    for k in range(kind_count):
        picked = picked + jnp.where(kind == 1.0 * k, dot_nn(pick, adj_s[k].astype(BF)), 0.0)
    link = dot_nt(pick, picked.astype(BF))
    eye = iota((keys, keys), 0) == iota((keys, keys), 1)
    clip_across = jnp.sum(jnp.where(eye, clip, 0.0), axis=0, keepdims=True)
    link = jnp.where(clip == clip_across, link, -1.0)
    tile = (iota((EP, heads * EQ), 1) % EQ == iota((EP, heads * EQ), 0)).astype(BF)
    return link[:, :half_slots], dot_nn(link[:, half_slots:].astype(BF), tile)


def stage_kernel(
    half_slots, guests, heads, nf, sb, count, flag_ref, send_ref, clip_ref, kind_ref, adj_ref, *refs
):
    link_ref, link_e_ref = refs[:2]
    ext_refs = refs[2 : 2 + count]
    adj_s = refs[-1]

    @pl.when(flag_ref[1] == count)
    def _():
        for j, ref in enumerate(ext_refs):
            ext_rows, hw = ref.shape
            pieces = [
                send_ref[(j * nf + f) * sb : (j * nf + f + 1) * sb, c : c + hw].astype(F32)[:guests]
                for c in range(0, send_ref.shape[1], hw)
                for f in range(nf)
            ]
            pieces.append(jnp.zeros((ext_rows - len(pieces) * guests, hw), F32))
            ref[...] = jnp.concatenate(pieces, axis=0).astype(BF)

    link, link_e = local_tables(
        half_slots, guests, heads, flag_ref[0], clip_ref, kind_ref, adj_ref, adj_s
    )
    link_ref[...] = link
    link_e_ref[...] = link_e


def frame_kernel(
    blocks,
    nf,
    sb,
    guests,
    *refs,
):
    (
        ext_ref,
        recv_ref,
        flag_ref,
        link_ref,
        link_e_ref,
        coef_ref,
        coef_e_ref,
        tok_ref,
        gain_ref,
        token_in_ref,
        w_hbm,
        out_s,
        pay_ref,
        sums_ref,
        x_s,
        xn_s,
        inv_s,
        hid_s,
        q_s,
        k_s,
        v_s,
        g_s,
        gu_s,
        gk_s,
        gv_s,
        ctx_s,
        gn_s,
        w_ref,
        sem,
    ) = refs
    d = gain_ref.shape[1]
    hw = w_ref.shape[1] // 3
    main = blocks * sb
    keys = main + EP
    rows = nf * main
    all_rows = rows + nf * EP
    heads = coef_ref.shape[0]
    hs = hw // heads
    seg_rows = nf * guests
    aligned = sb % 16 == 0

    copies = [pltpu.make_async_copy(w_hbm, w_ref, sem.at[0])]
    for cp in copies:
        cp.start()
    link = link_ref[...]
    link_e = link_e_ref[...]

    def gather(value):
        if aligned:
            return jnp.concatenate(
                [
                    value[(j * nf + f) * sb : (j * nf + f + 1) * sb]
                    for f in range(nf)
                    for j in range(blocks)
                ],
                axis=0,
            )
        r = iota((rows, 1), 0)
        slot = r % main
        source = ((slot // sb) * nf + r // main) * sb + slot % sb
        return dot_nn((iota((rows, rows), 1) == source).astype(BF), value).astype(BF)

    def scatter(value):
        if aligned:
            return jnp.concatenate(
                [
                    value[f * main + j * sb : f * main + (j + 1) * sb]
                    for j in range(blocks)
                    for f in range(nf)
                ],
                axis=0,
            )
        r = iota((rows, 1), 0)
        pair = r // sb
        source = (pair % nf) * main + (pair // nf) * sb + r % sb
        return dot_nn((iota((rows, rows), 1) == source).astype(BF), value).astype(BF)

    er = iota((nf * EP, 1), 0)
    guest_row = jnp.where(er % EP < guests, (er // EP) * guests + er % EP, 1 << 20)

    def guest_segment(seg):
        pick = (iota((nf * EP, ext_ref.shape[0]), 1) == guest_row + seg * seg_rows).astype(BF)
        return dot_nn(pick, ext_ref[...]).astype(BF)

    for c in range(d // hw):
        x_s[rows:, c * hw : (c + 1) * hw] = guest_segment(c)
    x_s[:rows] = gather(recv_ref[:, :d])
    tok = tok_ref[...]
    gain = gain_ref[...]
    for a in range(0, all_rows, 16):
        xb = x_s[a : a + 16]
        hid = xb[:, 0:1].astype(F32) > 0.5 * HIDDEN_MARK
        xf = jnp.where(hid, tok.astype(F32), xb.astype(F32))
        x_s[a : a + 16] = xf.astype(BF)
        inv = 1.0 / jnp.sqrt(jnp.mean(xf * xf, axis=1, keepdims=True) + 1e-6)
        inv_s[a : a + 16] = jnp.broadcast_to(inv, (16, 128))
        hid_s[a : a + 16] = jnp.broadcast_to(jnp.where(hid, 1.0, 0.0), (16, 128))
        xn_s[a : a + 16] = (xf * inv * gain).astype(BF)

    for cp in copies:
        cp.wait()
    for c, ref in enumerate((q_s, k_s, v_s)):
        part = dot_nn(xn_s[...], w_ref[:, c * hw : (c + 1) * hw]).astype(BF)
        if c == 0:
            part = part * BF(hs**-0.5)
        for f in range(nf):
            ref[f, :main] = part[f * main : (f + 1) * main]
            ref[f, main:] = part[rows + f * EP : rows + (f + 1) * EP]

    gc_main = gather(recv_ref[:, d:])
    gc_ext = guest_segment(d // hw)
    for f in range(nf):
        g_s[f, :main] = gc_main[f * main : (f + 1) * main]
        g_s[f, main:] = gc_ext[f * EP : (f + 1) * EP]

    own = (iota((heads * EQ, hw), 0) // EQ == iota((heads * EQ, hw), 1) // hs)
    bias_e = jnp.where(link_e < 0, MASKED, coef_e_ref[...] * link_e)
    coef_lanes = jnp.zeros((1, heads * EQ), F32)

    def spread(value):
        tall = jnp.concatenate([value] * heads, axis=0)
        return jnp.where(own, tall, jnp.zeros_like(tall))

    def fold(value):
        kept = jnp.where(own, value, 0.0)
        total = kept[0:EQ]
        for h in range(1, heads):
            total = total + kept[h * EQ : (h + 1) * EQ]
        return jnp.concatenate([total, jnp.zeros((EP - EQ, hw), F32)], axis=0)

    def attend(scores, grad_w):
        n = range(len(scores))
        top = [jnp.max(scores[i], axis=0, keepdims=True) for i in n]
        raw = [jnp.exp(scores[i] - top[i]) for i in n]
        w_t = [raw[i] * (1.0 / jnp.sum(raw[i], axis=0, keepdims=True)) for i in n]
        w_b = [w_t[i].astype(BF) for i in n]
        ds = [
            w_t[i] * (grad_w[i] - jnp.sum(w_t[i] * grad_w[i], axis=0, keepdims=True)) for i in n
        ]
        return w_t, w_b, ds, [ds[i].astype(BF) for i in n]

    fs = range(nf)
    q_e = [spread(q_s[f, main:].astype(F32)[:EQ]).astype(BF) for f in fs]
    g_e = [spread(g_s[f, main:].astype(F32)[:EQ]).astype(BF) for f in fs]
    s_t = [dot_nt(k_s[f], q_e[f]) + bias_e for f in fs]
    gw = [dot_nt(v_s[f], g_e[f]) for f in fs]
    w_t, w_b, ds, ds_b = attend(s_t, gw)
    for f in fs:
        coef_lanes = coef_lanes + jnp.sum(ds[f] * link_e, axis=0, keepdims=True)
    ctx_e = [dot_tn(w_b[f], v_s[f]) for f in fs]
    gq_e = [dot_tn(ds_b[f], k_s[f]) for f in fs]
    for f in fs:
        guest_rows = slice(rows + f * EP, rows + (f + 1) * EP)
        gk_s[f] = dot_nn(ds_b[f], q_e[f])
        gv_s[f] = dot_nn(w_b[f], g_e[f])
        ctx_s[guest_rows] = fold(ctx_e[f]).astype(BF)
        gu_s[guest_rows, :hw] = fold(gq_e[f] * hs**-0.5).astype(BF)

    lane = iota((1, 128), 1)
    coef_out = jnp.zeros((1, 128), F32)
    for h in range(heads):
        coef_out = coef_out + jnp.where(
            lane == h, jnp.sum(coef_lanes[:, h * EQ : (h + 1) * EQ]), 0.0
        )

    pair_w = 2 * hs
    low = iota((main, pair_w), 1) < hs
    zero = jnp.zeros((main, pair_w), BF)
    link_two = jnp.concatenate([link, link], axis=1)

    def two_heads(value):
        return jnp.concatenate(
            [jnp.where(low, value, zero), jnp.where(low, zero, value)], axis=0
        )

    for first_pair in range(0, heads // 2, 3):
        pairs = range(first_pair, min(first_pair + 3, heads // 2))
        items = [(p, f) for p in pairs for f in range(nf)]
        bias = {
            p: jnp.concatenate(
                [
                    jnp.where(link < 0, MASKED, coef_ref[2 * p] * link),
                    jnp.where(link < 0, MASKED, coef_ref[2 * p + 1] * link),
                ],
                axis=1,
            )
            for p in pairs
        }
        cols = {p: slice(p * pair_w, (p + 1) * pair_w) for p in pairs}
        k = [k_s[f, :, cols[p]] for p, f in items]
        v = [v_s[f, :, cols[p]] for p, f in items]
        qq = [two_heads(q_s[f, :main, cols[p]]) for p, f in items]
        gg = [two_heads(g_s[f, :main, cols[p]]) for p, f in items]
        s_t = [dot_nt(k[i], qq[i]) + bias[p] for i, (p, f) in enumerate(items)]
        gw = [dot_nt(v[i], gg[i]) for i in range(len(items))]
        w_t, w_b, ds, ds_b = attend(s_t, gw)
        ctx_t = [dot_tn(v[i], w_b[i]) for i in range(len(items))]
        gv = [gv_s[f, :, cols[p]] + dot_nn(w_b[i], gg[i]) for i, (p, f) in enumerate(items)]
        gq_t = [dot_tn(k[i], ds_b[i]) for i in range(len(items))]
        gk = [gk_s[f, :, cols[p]] + dot_nn(ds_b[i], qq[i]) for i, (p, f) in enumerate(items)]
        for i, (p, f) in enumerate(items):
            main_rows = slice(f * main, (f + 1) * main)
            guest_rows = slice(rows + f * EP, rows + (f + 1) * EP)
            both = jnp.concatenate([ctx_t[i][:hs, :main], ctx_t[i][hs:, main:]], axis=0)
            ctx_s[main_rows, cols[p]] = both.T.astype(BF)
            both = jnp.concatenate([gq_t[i][:hs, :main], gq_t[i][hs:, main:]], axis=0)
            gu_s[main_rows, cols[p]] = (both.T * hs**-0.5).astype(BF)
            for value, offset in ((gk[i].astype(BF), hw), (gv[i].astype(BF), 2 * hw)):
                here = slice(offset + p * pair_w, offset + (p + 1) * pair_w)
                gu_s[main_rows, here] = value[:main]
                gu_s[guest_rows, here] = value[main:]
        for p in pairs:
            ds_sum = functools.reduce(
                lambda x, y: x + y, [ds[i] for i, item in enumerate(items) if item[0] == p]
            )
            lanes = jnp.sum(ds_sum * link_two, axis=0, keepdims=True)
            coef_out = coef_out + jnp.where(lane == 2 * p, jnp.sum(lanes[:, :main]), 0.0)
            coef_out = coef_out + jnp.where(lane == 2 * p + 1, jnp.sum(lanes[:, main:]), 0.0)

    out_s[:, :hw] = scatter(ctx_s[:rows])

    gn_s[...] = dot_nt(gu_s[...], w_ref[...])
    guest_limit = jnp.where(flag_ref[0] == 1, guests, 0)
    main_limit = jnp.where(flag_ref[0] == 1, 0, guests)
    place = iota((16, 1), 0)
    token_sum = jnp.zeros((8, d), F32)
    gain_sum = jnp.zeros((8, d), F32)
    for a in range(0, all_rows, 16):
        gn = gn_s[a : a + 16]
        inv = inv_s[a : a + 16, 0:1]
        x_unit = x_s[a : a + 16].astype(F32) * inv
        g_gain = gn * gain
        gx = gn * x_unit
        mean_gx = jnp.mean(gx * gain, axis=1, keepdims=True)
        delta = (g_gain - x_unit * mean_gx) * inv
        if a >= rows:
            x_s[a : a + 16] = delta.astype(BF)
            valid = jnp.where(place < guest_limit, 1.0, 0.0)
        elif aligned:
            f, j = a // main, (a % main) // sb
            at = (j * nf + f) * sb + a % sb
            out_s[at : at + 16, hw : hw + d] = delta.astype(BF)
            valid = jnp.where(place + a % main >= main_limit, 1.0, 0.0)
        else:
            x_s[a : a + 16] = delta.astype(BF)
            valid = jnp.where(place + a % main >= main_limit, 1.0, 0.0)
        hid_valid = hid_s[a : a + 16, 0:1] * valid
        if a >= rows or a % main < guests:
            gx = gx * valid
        delta = delta * hid_valid
        gain_sum = gain_sum + (gx[:8] + gx[8:])
        token_sum = token_sum + (delta[:8] + delta[8:])
    if not aligned:
        out_s[:, hw : hw + d] = scatter(x_s[:rows])
    gain_sum = jnp.sum(gain_sum, axis=0, keepdims=True)
    token_sum = token_in_ref[...] + jnp.sum(token_sum, axis=0, keepdims=True)
    coef_row = jnp.concatenate([coef_out, jnp.zeros((1, hw - coef_out.shape[1]), F32)], axis=1)
    sums = jnp.concatenate(
        [token_sum[:, :hw], token_sum[:, hw:], gain_sum[:, :hw], gain_sum[:, hw:], coef_row]
        + [jnp.zeros((8 - SUMS, hw), F32)],
        axis=0,
    )
    high, low_part = split_two(sums)
    sums_ref[...] = high.astype(F32) + low_part.astype(F32)
    pair = jnp.concatenate([high.astype(F32), low_part.astype(F32)], axis=0).astype(BF)
    orow = iota((pay_ref.shape[0], 1), 0)
    k = orow - (1 + d // hw) * seg_rows
    source = jnp.where(
        k < 0, 1 << 20, jnp.where(k < SUMS, k, jnp.where(k < 2 * SUMS, k - SUMS + 8, 1 << 20))
    )
    total = dot_nn((iota((pay_ref.shape[0], 16), 1) == source).astype(BF), pair)
    inner = orow % seg_rows
    for s in range(1 + d // hw):
        piece = ctx_s[rows:] if s == 0 else x_s[rows:, (s - 1) * hw : s * hw]
        source = jnp.where(
            orow // seg_rows == s, (inner // guests) * EP + inner % guests, 1 << 20
        )
        total = total + dot_nn(
            (iota((pay_ref.shape[0], nf * EP), 1) == source).astype(BF), piece
        )
    pay_ref[...] = total.astype(BF)


VMEM = pl.BlockSpec(memory_space=pltpu.VMEM)
SMEM = pl.BlockSpec(memory_space=pltpu.SMEM)
HBM = pl.BlockSpec(memory_space=pl.ANY)


def on_device(
    n,
    joints_x,
    cotangent,
    hidden,
    stream_clip,
    stream_kind,
    adjacency,
    mask_token,
    norm_gain,
    w_qkv,
    w_out,
    graph_coef,
):
    _, slots, frames, d = joints_x.shape
    hw = w_out.shape[0]
    heads = graph_coef.shape[0]
    total = stream_clip.shape[1]
    half = n // 2
    nf = frames // half
    half_slots = total // 2
    guests = BIG_CLIP - half_slots
    rows = slots * frames
    wide = d + hw
    segs = wide // hw
    me = lax.axis_index("seq")
    first_half = me < half
    groups = [list(range(half)), list(range(half, n))]

    x = joints_x.reshape(rows, d)
    cot = cotangent.reshape(rows, d)
    hid = hidden[0]
    tok = mask_token.reshape(1, d)
    flag = jnp.stack([first_half.astype(jnp.int32), me])

    send, token_cot = pl.pallas_call(
        functools.partial(send_kernel, slots, frames),
        out_shape=(
            jax.ShapeDtypeStruct((rows, wide), BF),
            jax.ShapeDtypeStruct((1, d), F32),
        ),
        in_specs=[HBM] * 4,
        out_specs=(VMEM, VMEM),
        scratch_shapes=[
            pltpu.VMEM((rows, d), BF),
            pltpu.VMEM((rows, d), BF),
            pltpu.VMEM(hid.shape, jnp.int32),
            pltpu.VMEM(w_out.shape, BF),
            pltpu.SemaphoreType.DMA((4,)),
        ],
        compiler_params=pltpu.CompilerParams(vmem_limit_bytes=SEND_LIMIT),
        name="send",
    )(x, cot, hid, w_out)

    recv = lax.all_to_all(send, "seq", 0, 0, axis_index_groups=groups, tiled=True)

    def buffer_row(f, e):
        return ((e // slots) * nf + f) * slots + e % slots

    run = min(slots, guests)
    starts = [
        (buffer_row(f, e), min(run, guests - e)) for f in range(nf) for e in range(0, guests, run)
    ]
    ext_rows = -(-segs * nf * guests // 16) * 16
    direct = slots >= guests and slots % 16 == 0 and half <= 8
    joint_pad = -(-adjacency.shape[1] // 256) * 256
    keys = half_slots + EP
    count = half if direct else 0
    link, link_e, *packed = pl.pallas_call(
        functools.partial(stage_kernel, half_slots, guests, heads, nf, slots, count),
        out_shape=(
            jax.ShapeDtypeStruct((keys, half_slots), F32),
            jax.ShapeDtypeStruct((keys, heads * EQ), F32),
        )
        + (jax.ShapeDtypeStruct((ext_rows, hw), BF),) * count,
        in_specs=[SMEM] + [VMEM] * 4,
        out_specs=(VMEM,) * (2 + count),
        scratch_shapes=[pltpu.VMEM((adjacency.shape[0], joint_pad, joint_pad), F32)],
        compiler_params=pltpu.CompilerParams(vmem_limit_bytes=VMEM_LIMIT),
        name="stage",
    )(flag, send, stream_clip, stream_kind, adjacency)
    if direct:
        ext = lax.ppermute(packed[0], "seq", [(half, 0)])
        for j in range(1, half):
            ext = ext + lax.ppermute(packed[j], "seq", [(half, j)])
    else:
        pieces = [
            recv[a : a + c, s * hw : (s + 1) * hw] for s in range(segs) for a, c in starts
        ]
        pieces.append(jnp.zeros((ext_rows - segs * nf * guests, hw), BF))
        ext = lax.ppermute(
            jnp.concatenate(pieces, axis=0), "seq", [(half + i, i) for i in range(half)]
        )

    main = half_slots
    all_rows = rows + nf * EP
    block_rows = nf * slots
    shared = block_rows % 32 == 0
    out_wide = wide + (LANES if shared else 0)
    head_rows = -(-guests // slots) * block_rows
    head_rows = -(-head_rows // 16) * 16
    pay_rows = -(-(segs * nf * guests + 2 * SUMS) // 8) * 8
    per_frame = (nf, main + EP, hw)
    out, pay, own_sums = pl.pallas_call(
        functools.partial(frame_kernel, half, nf, slots, guests),
        out_shape=(
            jax.ShapeDtypeStruct((rows, out_wide), BF),
            jax.ShapeDtypeStruct((pay_rows, hw), BF),
            jax.ShapeDtypeStruct((8, hw), F32),
        ),
        in_specs=[VMEM, VMEM, SMEM, VMEM, VMEM, SMEM, VMEM, VMEM, VMEM, VMEM, HBM],
        out_specs=(VMEM, VMEM, VMEM),
        scratch_shapes=[
            pltpu.VMEM((all_rows, d), BF),
            pltpu.VMEM((all_rows, d), BF),
            pltpu.VMEM((all_rows, 128), F32),
            pltpu.VMEM((all_rows, 128), F32),
            pltpu.VMEM(per_frame, BF),
            pltpu.VMEM(per_frame, BF),
            pltpu.VMEM(per_frame, BF),
            pltpu.VMEM(per_frame, BF),
            pltpu.VMEM((all_rows, 3 * hw), BF),
            pltpu.VMEM(per_frame, F32),
            pltpu.VMEM(per_frame, F32),
            pltpu.VMEM((all_rows, hw), BF),
            pltpu.VMEM((all_rows, d), F32),
            pltpu.VMEM((d, 3 * hw), BF),
            pltpu.SemaphoreType.DMA((3,)),
        ],
        compiler_params=pltpu.CompilerParams(vmem_limit_bytes=FRAMES_LIMIT),
        name="frames",
    )(
        ext,
        recv,
        flag,
        link,
        link_e,
        graph_coef,
        jnp.repeat(graph_coef, EQ).reshape(1, heads * EQ),
        tok,
        norm_gain.reshape(1, d),
        token_cot,
        w_qkv,
    )

    flip = [(i, (i + half) % n) for i in range(n)]
    got = lax.ppermute(pay, "seq", flip)
    core = lax.ppermute(own_sums, "dp", [(0, 1), (1, 0)])
    cross = lax.ppermute(
        own_sums, ("dp", "seq"), [(c * n + i, (1 - c) * n + j) for c in range(2) for i, j in flip]
    )
    merged, sums = pl.pallas_call(
        functools.partial(merge_kernel, nf, slots, guests, wide, head_rows),
        out_shape=(
            jax.ShapeDtypeStruct((rows, out_wide), BF),
            jax.ShapeDtypeStruct((8, hw), F32),
        ),
        in_specs=[SMEM] + [VMEM] * 5,
        out_specs=(VMEM, VMEM),
        input_output_aliases={1: 0},
        compiler_params=pltpu.CompilerParams(vmem_limit_bytes=VMEM_LIMIT),
        name="merge",
    )(flag, out, own_sums, got, core, cross)
    returned = lax.all_to_all(merged, "seq", 0, 0, axis_index_groups=groups, tiled=True)

    if not shared:
        k = 1
        while k < half:
            sums = sums + lax.ppermute(sums, "seq", [(i, i ^ k) for i in range(n)])
            k *= 2

    layer_out, grad_x, token, gain, coef = pl.pallas_call(
        functools.partial(final_kernel, slots, frames, shared),
        out_shape=(
            jax.ShapeDtypeStruct((rows, d), BF),
            jax.ShapeDtypeStruct((rows, d), BF),
            jax.ShapeDtypeStruct((d,), F32),
            jax.ShapeDtypeStruct((d,), F32),
            jax.ShapeDtypeStruct((1, heads), F32),
        ),
        in_specs=[VMEM, HBM, HBM, VMEM, VMEM, VMEM, VMEM],
        out_specs=(HBM, HBM, VMEM, VMEM, VMEM),
        scratch_shapes=[
            pltpu.VMEM((rows, d), BF),
            pltpu.VMEM((rows, d), BF),
            pltpu.VMEM((rows, d), BF),
            pltpu.VMEM((rows, d), BF),
            pltpu.SemaphoreType.DMA((6,)),
        ],
        compiler_params=pltpu.CompilerParams(vmem_limit_bytes=VMEM_LIMIT),
        name="final",
    )(returned, x, cot, hid, tok, w_out, sums)

    shape = (1, slots, frames, d)
    return (
        layer_out.reshape(shape),
        grad_x.reshape(shape),
        token,
        gain,
        coef.reshape(-1),
    )


def solution(mesh):
    return jax.shard_map(
        functools.partial(on_device, mesh.shape["seq"]),
        mesh=mesh,
        in_specs=(
            P("dp", "seq", None, None),
            P("dp", "seq", None, None),
            P("dp", "seq", None),
            P("dp", None),
            P("dp", None),
            P(),
            P(),
            P(),
            P(),
            P(),
            P(),
        ),
        out_specs=(P("dp", "seq", None, None), P("dp", "seq", None, None), P(), P(), P()),
        check_vma=False,
    )
```

```python
import functools

import jax
import jax.numpy as jnp
import numpy as np
from jax import lax
from jax.experimental import pallas as pl
from jax.experimental.pallas import tpu as pltpu
from jax.sharding import PartitionSpec as P

BF = jnp.bfloat16
F32 = jnp.float32
BIG_CLIP = 133
HIDDEN_MARK = 64.0
MASKED = -1e30
EP = 16
EQ = 8
VMEM_LIMIT = 16 << 20
FRAMES_LIMIT = 50 << 20
SEND_LIMIT = 56 << 20
SUMS = 5
LANES = 256


def dot_nn(a, b):
    return lax.dot_general(a, b, (((1,), (0,)), ((), ())), preferred_element_type=F32)


def dot_nt(a, b):
    return lax.dot_general(a, b, (((1,), (1,)), ((), ())), preferred_element_type=F32)


def dot_tn(a, b):
    return lax.dot_general(a, b, (((0,), (0,)), ((), ())), preferred_element_type=F32)


def iota(shape, axis):
    return lax.broadcasted_iota(jnp.int32, shape, axis)


def hidden_column(hid, slots, frames, frame_major):
    rows = slots * frames
    r = iota((rows, 1), 0)
    slot_of = r % slots if frame_major else r // frames
    frame_of = r // slots if frame_major else r % frames
    pick_slot = (slot_of == iota((rows, slots), 1)).astype(BF)
    by_slot = dot_nn(pick_slot, hid.astype(F32).astype(BF))
    return jnp.sum(jnp.where(frame_of == iota((rows, frames), 1), by_slot, 0.0), axis=1, keepdims=True)


def row_swap(slots, frames, to_frame_major):
    rows = slots * frames
    r = iota((rows, 1), 0)
    if to_frame_major:
        source = (r % slots) * frames + r // slots
    else:
        source = (r % frames) * slots + r // frames
    return (iota((rows, rows), 1) == source).astype(BF)


def send_kernel(
    slots,
    frames,
    x_hbm,
    cot_hbm,
    hid_hbm,
    w_out_hbm,
    out_ref,
    token_ref,
    x_ref,
    cot_ref,
    hid_ref,
    w_ref,
    sem,
):
    width = x_ref.shape[1]
    copies = [
        pltpu.make_async_copy(hid_hbm, hid_ref, sem.at[0]),
        pltpu.make_async_copy(x_hbm, x_ref, sem.at[1]),
        pltpu.make_async_copy(cot_hbm, cot_ref, sem.at[2]),
        pltpu.make_async_copy(w_out_hbm, w_ref, sem.at[3]),
    ]
    for cp in copies:
        cp.start()
    swap = row_swap(slots, frames, True)
    copies[0].wait()
    hid_t = hidden_column(hid_ref[...], slots, frames, True)
    hid_s = hidden_column(hid_ref[...], slots, frames, False)
    copies[1].wait()
    moved = dot_nn(swap, x_ref[...])
    first = jnp.where(
        (iota((moved.shape[0], 128), 1) == 0) & (hid_t > 0.5), HIDDEN_MARK, moved[:, :128]
    )
    out_ref[:, :128] = first.astype(BF)
    out_ref[:, 128:width] = moved[:, 128:].astype(BF)
    copies[2].wait()
    token_ref[...] = jnp.sum(
        jnp.where(hid_s > 0.5, cot_ref[...].astype(F32), 0.0), axis=0, keepdims=True
    )
    copies[3].wait()
    gc = dot_nt(cot_ref[...], w_ref[...]).astype(BF)
    out_ref[:, width:] = dot_nn(swap, gc).astype(BF)


def final_kernel(
    slots,
    frames,
    recv_ref,
    x_hbm,
    cot_hbm,
    hid_ref,
    tok_ref,
    w_ref,
    out_hbm,
    grad_hbm,
    x_ref,
    cot_ref,
    out_s,
    grad_s,
    sem,
):
    hw, d = w_ref.shape
    wide = hw + d
    copies = [
        pltpu.make_async_copy(cot_hbm, cot_ref, sem.at[0]),
        pltpu.make_async_copy(x_hbm, x_ref, sem.at[1]),
    ]
    for cp in copies:
        cp.start()
    swap = row_swap(slots, frames, False)
    hid = hidden_column(hid_ref[...], slots, frames, False) > 0.5
    ctx = dot_nn(swap, recv_ref[:, :hw]).astype(BF)
    attn = dot_nn(ctx, w_ref[...]).astype(BF)
    delta = dot_nn(swap, recv_ref[:, hw:wide])
    for cp in copies:
        cp.wait()
    stores = []
    half = swap.shape[0] // 2
    for h in range(2):
        r = slice(h * half, (h + 1) * half)
        here = pl.ds(h * half, half)
        grad_s[r] = jnp.where(hid[r], 0.0, cot_ref[r].astype(F32) + delta[r]).astype(BF)
        stores.append(pltpu.make_async_copy(grad_s.at[here], grad_hbm.at[here], sem.at[2 + 2 * h]))
        stores[-1].start()
        x_in = jnp.where(hid[r], tok_ref[...].astype(F32), x_ref[r].astype(F32))
        out_s[r] = (x_in + attn[r].astype(F32)).astype(BF)
        stores.append(pltpu.make_async_copy(out_s.at[here], out_hbm.at[here], sem.at[3 + 2 * h]))
        stores[-1].start()
    for cp in stores:
        cp.wait()


def sums_kernel(here_ref, core_ref, token_ref, gain_ref, coef_ref):
    total = here_ref[...] + core_ref[...]
    width = total.shape[1]
    parts = token_ref.shape[0] // width
    for c in range(parts):
        at = pl.ds(c * width, width)
        token_ref[at] = total[c : c + 1].reshape(width)
        gain_ref[at] = total[parts + c : parts + c + 1].reshape(width)
    coef_ref[...] = total[2 * parts : 2 * parts + 1, : coef_ref.shape[1]]


def split_two(value):
    high = value.astype(BF)
    return high, (value - high.astype(F32)).astype(BF)


def merge_kernel(
    nf, sb, guests, wide, head_rows, flag_ref, buf_ref, own_ref, got_ref, out_ref, *sums_ref
):
    hw = got_ref.shape[1]
    segs = wide // hw
    seg_rows = nf * guests
    total_rows = out_ref.shape[0]
    i = iota((8, got_ref.shape[0]), 0)
    k = iota((8, got_ref.shape[0]), 1) - segs * seg_rows
    pick = ((i < SUMS) & ((k == i) | (k == i + SUMS))).astype(BF)
    sums = own_ref[...] + dot_nn(pick, got_ref[...])
    if sums_ref:
        sums_ref[0][...] = sums
    if out_ref.shape[1] > wide:
        flat = jnp.concatenate(
            [sums[a : a + 1, c : c + LANES] for a in range(SUMS) for c in range(0, hw, LANES)]
            + [jnp.zeros((1, LANES), F32)],
            axis=0,
        )
        block = jnp.concatenate(split_two(flat), axis=0)
        for j in range(total_rows // block.shape[0]):
            out_ref[j * block.shape[0] : (j + 1) * block.shape[0], wide:] = block
    r = iota((head_rows, 1), 0)
    slot = (r // (nf * sb)) * sb + r % sb
    from_row = ((r // sb) % nf) * guests + slot
    guest = jnp.where(slot < guests, 1, 0)
    take = guest * jnp.where(flag_ref[0] == 1, 0, 1)
    for s in range(segs):
        source = jnp.where(guest == 1, s * seg_rows + from_row, 1 << 20)
        pick = (iota((head_rows, got_ref.shape[0]), 1) == source).astype(BF)
        here = slice(s * hw, (s + 1) * hw)
        out_ref[:head_rows, here] = jnp.where(
            take == 1, dot_nn(pick, got_ref[...]), buf_ref[:head_rows, here].astype(F32)
        ).astype(BF)


def local_tables(half_slots, guests, heads, first_half, clip_ref, kind_ref, adj_ref, adj_s):
    total = clip_ref.shape[1]
    kind_count, joint_max = adj_ref.shape[0], adj_ref.shape[1]
    keys = half_slots + EP
    adj_s[...] = jnp.zeros(adj_s.shape, F32)
    adj_s[:, :joint_max, :joint_max] = adj_ref[...].astype(F32)
    i = iota((keys, 1), 0)
    slot = jnp.where(i < half_slots, i + jnp.where(first_half == 1, 0, half_slots), i)
    valid = ((i < half_slots) & (i >= jnp.where(first_half == 1, 0, guests))) | (
        (i >= half_slots) & (i < jnp.where(first_half == 1, half_slots + guests, 0))
    )
    lanes = iota((keys, total), 1)
    at = lanes == slot
    clip_row = clip_ref[...].astype(F32)
    clip = jnp.sum(jnp.where(at, clip_row, 0.0), axis=1, keepdims=True)
    kind = jnp.sum(jnp.where(at, kind_ref[...].astype(F32), 0.0), axis=1, keepdims=True)
    first = jnp.min(
        jnp.where(clip_row == clip, lanes.astype(F32), 1.0 * total), axis=1, keepdims=True
    )
    joint = slot.astype(F32) - first
    clip = jnp.where(valid, clip, -1.0 - i.astype(F32))
    pick = (iota((keys, adj_s.shape[1]), 1).astype(F32) == joint).astype(BF)
    picked = jnp.zeros((keys, adj_s.shape[2]), F32)
    for k in range(kind_count):
        picked = picked + jnp.where(kind == 1.0 * k, dot_nn(pick, adj_s[k].astype(BF)), 0.0)
    link = dot_nt(pick, picked.astype(BF))
    eye = iota((keys, keys), 0) == iota((keys, keys), 1)
    clip_across = jnp.sum(jnp.where(eye, clip, 0.0), axis=0, keepdims=True)
    link = jnp.where(clip == clip_across, link, -1.0)
    tile = (iota((EP, heads * EQ), 1) % EQ == iota((EP, heads * EQ), 0)).astype(BF)
    return link[:, :half_slots], dot_nn(link[:, half_slots:].astype(BF), tile)


def stage_kernel(
    half_slots, guests, heads, nf, sb, count, flag_ref, send_ref, clip_ref, kind_ref, adj_ref, *refs
):
    link_ref, link_e_ref = refs[:2]
    ext_refs = refs[2 : 2 + count]
    adj_s = refs[-1]

    @pl.when(flag_ref[1] == count)
    def _():
        for j, ref in enumerate(ext_refs):
            ext_rows, hw = ref.shape
            pieces = [
                send_ref[(j * nf + f) * sb : (j * nf + f + 1) * sb, c : c + hw].astype(F32)[:guests]
                for c in range(0, send_ref.shape[1], hw)
                for f in range(nf)
            ]
            pieces.append(jnp.zeros((ext_rows - len(pieces) * guests, hw), F32))
            ref[...] = jnp.concatenate(pieces, axis=0).astype(BF)

    link, link_e = local_tables(
        half_slots, guests, heads, flag_ref[0], clip_ref, kind_ref, adj_ref, adj_s
    )
    link_ref[...] = link
    link_e_ref[...] = link_e


def frame_kernel(
    blocks,
    nf,
    sb,
    guests,
    *refs,
):
    (
        ext_ref,
        recv_ref,
        flag_ref,
        link_ref,
        link_e_ref,
        coef_ref,
        coef_e_ref,
        tok_ref,
        gain_ref,
        token_in_ref,
        w_hbm,
        out_s,
        pay_ref,
        sums_ref,
        x_s,
        xn_s,
        inv_s,
        hid_s,
        q_s,
        k_s,
        v_s,
        g_s,
        gu_s,
        gk_s,
        gv_s,
        ctx_s,
        gn_s,
        w_ref,
        sem,
    ) = refs
    d = gain_ref.shape[1]
    hw = w_ref.shape[1] // 3
    main = blocks * sb
    keys = main + EP
    rows = nf * main
    all_rows = rows + nf * EP
    heads = coef_ref.shape[0]
    hs = hw // heads
    seg_rows = nf * guests
    aligned = sb % 16 == 0

    copies = [pltpu.make_async_copy(w_hbm, w_ref, sem.at[0])]
    for cp in copies:
        cp.start()
    link = link_ref[...]
    link_e = link_e_ref[...]

    def gather(value):
        if aligned:
            return jnp.concatenate(
                [
                    value[(j * nf + f) * sb : (j * nf + f + 1) * sb]
                    for f in range(nf)
                    for j in range(blocks)
                ],
                axis=0,
            )
        r = iota((rows, 1), 0)
        slot = r % main
        source = ((slot // sb) * nf + r // main) * sb + slot % sb
        return dot_nn((iota((rows, rows), 1) == source).astype(BF), value).astype(BF)

    def scatter(value):
        if aligned:
            return jnp.concatenate(
                [
                    value[f * main + j * sb : f * main + (j + 1) * sb]
                    for j in range(blocks)
                    for f in range(nf)
                ],
                axis=0,
            )
        r = iota((rows, 1), 0)
        pair = r // sb
        source = (pair % nf) * main + (pair // nf) * sb + r % sb
        return dot_nn((iota((rows, rows), 1) == source).astype(BF), value).astype(BF)

    er = iota((nf * EP, 1), 0)
    guest_row = jnp.where(er % EP < guests, (er // EP) * guests + er % EP, 1 << 20)

    def guest_segment(seg):
        pick = (iota((nf * EP, ext_ref.shape[0]), 1) == guest_row + seg * seg_rows).astype(BF)
        return dot_nn(pick, ext_ref[...]).astype(BF)

    for c in range(d // hw):
        x_s[rows:, c * hw : (c + 1) * hw] = guest_segment(c)
    x_s[:rows] = gather(recv_ref[:, :d])
    tok = tok_ref[...]
    gain = gain_ref[...]
    for a in range(0, all_rows, 16):
        xb = x_s[a : a + 16]
        hid = xb[:, 0:1].astype(F32) > 0.5 * HIDDEN_MARK
        xf = jnp.where(hid, tok.astype(F32), xb.astype(F32))
        x_s[a : a + 16] = xf.astype(BF)
        inv = 1.0 / jnp.sqrt(jnp.mean(xf * xf, axis=1, keepdims=True) + 1e-6)
        inv_s[a : a + 16] = jnp.broadcast_to(inv, (16, 128))
        hid_s[a : a + 16] = jnp.broadcast_to(jnp.where(hid, 1.0, 0.0), (16, 128))
        xn_s[a : a + 16] = (xf * inv * gain).astype(BF)

    for cp in copies:
        cp.wait()
    for c, ref in enumerate((q_s, k_s, v_s)):
        part = dot_nn(xn_s[...], w_ref[:, c * hw : (c + 1) * hw]).astype(BF)
        if c == 0:
            part = part * BF(hs**-0.5)
        for f in range(nf):
            ref[f, :main] = part[f * main : (f + 1) * main]
            ref[f, main:] = part[rows + f * EP : rows + (f + 1) * EP]

    gc_main = gather(recv_ref[:, d:])
    gc_ext = guest_segment(d // hw)
    for f in range(nf):
        g_s[f, :main] = gc_main[f * main : (f + 1) * main]
        g_s[f, main:] = gc_ext[f * EP : (f + 1) * EP]

    own = (iota((heads * EQ, hw), 0) // EQ == iota((heads * EQ, hw), 1) // hs)
    bias_e = jnp.where(link_e < 0, MASKED, coef_e_ref[...] * link_e)
    coef_lanes = jnp.zeros((1, heads * EQ), F32)

    def spread(value):
        tall = jnp.concatenate([value] * heads, axis=0)
        return jnp.where(own, tall, jnp.zeros_like(tall))

    def fold(value):
        kept = jnp.where(own, value, 0.0)
        total = kept[0:EQ]
        for h in range(1, heads):
            total = total + kept[h * EQ : (h + 1) * EQ]
        return jnp.concatenate([total, jnp.zeros((EP - EQ, hw), F32)], axis=0)

    def attend(scores, grad_w):
        n = range(len(scores))
        top = [jnp.max(scores[i], axis=0, keepdims=True) for i in n]
        raw = [jnp.exp(scores[i] - top[i]) for i in n]
        w_t = [raw[i] * (1.0 / jnp.sum(raw[i], axis=0, keepdims=True)) for i in n]
        w_b = [w_t[i].astype(BF) for i in n]
        ds = [
            w_t[i] * (grad_w[i] - jnp.sum(w_t[i] * grad_w[i], axis=0, keepdims=True)) for i in n
        ]
        return w_t, w_b, ds, [ds[i].astype(BF) for i in n]

    fs = range(nf)
    q_e = [spread(q_s[f, main:].astype(F32)[:EQ]).astype(BF) for f in fs]
    g_e = [spread(g_s[f, main:].astype(F32)[:EQ]).astype(BF) for f in fs]
    s_t = [dot_nt(k_s[f], q_e[f]) + bias_e for f in fs]
    gw = [dot_nt(v_s[f], g_e[f]) for f in fs]
    w_t, w_b, ds, ds_b = attend(s_t, gw)
    for f in fs:
        coef_lanes = coef_lanes + jnp.sum(ds[f] * link_e, axis=0, keepdims=True)
    ctx_e = [dot_tn(w_b[f], v_s[f]) for f in fs]
    gq_e = [dot_tn(ds_b[f], k_s[f]) for f in fs]
    for f in fs:
        guest_rows = slice(rows + f * EP, rows + (f + 1) * EP)
        gk_s[f] = dot_nn(ds_b[f], q_e[f])
        gv_s[f] = dot_nn(w_b[f], g_e[f])
        ctx_s[guest_rows] = fold(ctx_e[f]).astype(BF)
        gu_s[guest_rows, :hw] = fold(gq_e[f] * hs**-0.5).astype(BF)

    lane = iota((1, 128), 1)
    coef_out = jnp.zeros((1, 128), F32)
    for h in range(heads):
        coef_out = coef_out + jnp.where(
            lane == h, jnp.sum(coef_lanes[:, h * EQ : (h + 1) * EQ]), 0.0
        )

    pair_w = 2 * hs
    low = iota((main, pair_w), 1) < hs
    zero = jnp.zeros((main, pair_w), BF)
    link_two = jnp.concatenate([link, link], axis=1)

    def two_heads(value):
        return jnp.concatenate(
            [jnp.where(low, value, zero), jnp.where(low, zero, value)], axis=0
        )

    for first_pair in range(0, heads // 2, 3):
        pairs = range(first_pair, min(first_pair + 3, heads // 2))
        items = [(p, f) for p in pairs for f in range(nf)]
        bias = {
            p: jnp.concatenate(
                [
                    jnp.where(link < 0, MASKED, coef_ref[2 * p] * link),
                    jnp.where(link < 0, MASKED, coef_ref[2 * p + 1] * link),
                ],
                axis=1,
            )
            for p in pairs
        }
        cols = {p: slice(p * pair_w, (p + 1) * pair_w) for p in pairs}
        k = [k_s[f, :, cols[p]] for p, f in items]
        v = [v_s[f, :, cols[p]] for p, f in items]
        qq = [two_heads(q_s[f, :main, cols[p]]) for p, f in items]
        gg = [two_heads(g_s[f, :main, cols[p]]) for p, f in items]
        s_t = [dot_nt(k[i], qq[i]) + bias[p] for i, (p, f) in enumerate(items)]
        gw = [dot_nt(v[i], gg[i]) for i in range(len(items))]
        w_t, w_b, ds, ds_b = attend(s_t, gw)
        ctx_t = [dot_tn(v[i], w_b[i]) for i in range(len(items))]
        gv = [gv_s[f, :, cols[p]] + dot_nn(w_b[i], gg[i]) for i, (p, f) in enumerate(items)]
        gq_t = [dot_tn(k[i], ds_b[i]) for i in range(len(items))]
        gk = [gk_s[f, :, cols[p]] + dot_nn(ds_b[i], qq[i]) for i, (p, f) in enumerate(items)]
        for i, (p, f) in enumerate(items):
            main_rows = slice(f * main, (f + 1) * main)
            guest_rows = slice(rows + f * EP, rows + (f + 1) * EP)
            both = jnp.concatenate([ctx_t[i][:hs, :main], ctx_t[i][hs:, main:]], axis=0)
            ctx_s[main_rows, cols[p]] = both.T.astype(BF)
            both = jnp.concatenate([gq_t[i][:hs, :main], gq_t[i][hs:, main:]], axis=0)
            gu_s[main_rows, cols[p]] = (both.T * hs**-0.5).astype(BF)
            for value, offset in ((gk[i].astype(BF), hw), (gv[i].astype(BF), 2 * hw)):
                here = slice(offset + p * pair_w, offset + (p + 1) * pair_w)
                gu_s[main_rows, here] = value[:main]
                gu_s[guest_rows, here] = value[main:]
        for p in pairs:
            ds_sum = functools.reduce(
                lambda x, y: x + y, [ds[i] for i, item in enumerate(items) if item[0] == p]
            )
            lanes = jnp.sum(ds_sum * link_two, axis=0, keepdims=True)
            coef_out = coef_out + jnp.where(lane == 2 * p, jnp.sum(lanes[:, :main]), 0.0)
            coef_out = coef_out + jnp.where(lane == 2 * p + 1, jnp.sum(lanes[:, main:]), 0.0)

    out_s[:, :hw] = scatter(ctx_s[:rows])

    gn_s[...] = dot_nt(gu_s[...], w_ref[...])
    guest_limit = jnp.where(flag_ref[0] == 1, guests, 0)
    main_limit = jnp.where(flag_ref[0] == 1, 0, guests)
    place = iota((16, 1), 0)
    token_sum = jnp.zeros((8, d), F32)
    gain_sum = jnp.zeros((8, d), F32)
    for a in range(0, all_rows, 16):
        gn = gn_s[a : a + 16]
        inv = inv_s[a : a + 16, 0:1]
        x_unit = x_s[a : a + 16].astype(F32) * inv
        g_gain = gn * gain
        gx = gn * x_unit
        mean_gx = jnp.mean(gx * gain, axis=1, keepdims=True)
        delta = (g_gain - x_unit * mean_gx) * inv
        if a >= rows:
            x_s[a : a + 16] = delta.astype(BF)
            valid = jnp.where(place < guest_limit, 1.0, 0.0)
        elif aligned:
            f, j = a // main, (a % main) // sb
            at = (j * nf + f) * sb + a % sb
            out_s[at : at + 16, hw : hw + d] = delta.astype(BF)
            valid = jnp.where(place + a % main >= main_limit, 1.0, 0.0)
        else:
            x_s[a : a + 16] = delta.astype(BF)
            valid = jnp.where(place + a % main >= main_limit, 1.0, 0.0)
        hid_valid = hid_s[a : a + 16, 0:1] * valid
        if a >= rows or a % main < guests:
            gx = gx * valid
        delta = delta * hid_valid
        gain_sum = gain_sum + (gx[:8] + gx[8:])
        token_sum = token_sum + (delta[:8] + delta[8:])
    if not aligned:
        out_s[:, hw : hw + d] = scatter(x_s[:rows])
    gain_sum = jnp.sum(gain_sum, axis=0, keepdims=True)
    token_sum = token_in_ref[...] + jnp.sum(token_sum, axis=0, keepdims=True)
    coef_row = jnp.concatenate([coef_out, jnp.zeros((1, hw - coef_out.shape[1]), F32)], axis=1)
    sums = jnp.concatenate(
        [token_sum[:, :hw], token_sum[:, hw:], gain_sum[:, :hw], gain_sum[:, hw:], coef_row]
        + [jnp.zeros((8 - SUMS, hw), F32)],
        axis=0,
    )
    high, low_part = split_two(sums)
    sums_ref[...] = high.astype(F32) + low_part.astype(F32)
    pair = jnp.concatenate([high.astype(F32), low_part.astype(F32)], axis=0).astype(BF)
    orow = iota((pay_ref.shape[0], 1), 0)
    k = orow - (1 + d // hw) * seg_rows
    source = jnp.where(
        k < 0, 1 << 20, jnp.where(k < SUMS, k, jnp.where(k < 2 * SUMS, k - SUMS + 8, 1 << 20))
    )
    total = dot_nn((iota((pay_ref.shape[0], 16), 1) == source).astype(BF), pair)
    inner = orow % seg_rows
    for s in range(1 + d // hw):
        piece = ctx_s[rows:] if s == 0 else x_s[rows:, (s - 1) * hw : s * hw]
        source = jnp.where(
            orow // seg_rows == s, (inner // guests) * EP + inner % guests, 1 << 20
        )
        total = total + dot_nn(
            (iota((pay_ref.shape[0], nf * EP), 1) == source).astype(BF), piece
        )
    pay_ref[...] = total.astype(BF)


VMEM = pl.BlockSpec(memory_space=pltpu.VMEM)
SMEM = pl.BlockSpec(memory_space=pltpu.SMEM)
HBM = pl.BlockSpec(memory_space=pl.ANY)


def on_device(
    n,
    joints_x,
    cotangent,
    hidden,
    stream_clip,
    stream_kind,
    adjacency,
    mask_token,
    norm_gain,
    w_qkv,
    w_out,
    graph_coef,
):
    _, slots, frames, d = joints_x.shape
    hw = w_out.shape[0]
    heads = graph_coef.shape[0]
    total = stream_clip.shape[1]
    half = n // 2
    nf = frames // half
    half_slots = total // 2
    guests = BIG_CLIP - half_slots
    rows = slots * frames
    wide = d + hw
    segs = wide // hw
    me = lax.axis_index("seq")
    first_half = me < half
    groups = [list(range(half)), list(range(half, n))]

    x = joints_x.reshape(rows, d)
    cot = cotangent.reshape(rows, d)
    hid = hidden[0]
    tok = mask_token.reshape(1, d)
    flag = jnp.stack([first_half.astype(jnp.int32), me])

    send, token_cot = pl.pallas_call(
        functools.partial(send_kernel, slots, frames),
        out_shape=(
            jax.ShapeDtypeStruct((rows, wide), BF),
            jax.ShapeDtypeStruct((1, d), F32),
        ),
        in_specs=[HBM] * 4,
        out_specs=(VMEM, VMEM),
        scratch_shapes=[
            pltpu.VMEM((rows, d), BF),
            pltpu.VMEM((rows, d), BF),
            pltpu.VMEM(hid.shape, jnp.int32),
            pltpu.VMEM(w_out.shape, BF),
            pltpu.SemaphoreType.DMA((4,)),
        ],
        compiler_params=pltpu.CompilerParams(vmem_limit_bytes=SEND_LIMIT),
        name="send",
    )(x, cot, hid, w_out)

    recv = lax.all_to_all(send, "seq", 0, 0, axis_index_groups=groups, tiled=True)

    def buffer_row(f, e):
        return ((e // slots) * nf + f) * slots + e % slots

    run = min(slots, guests)
    starts = [
        (buffer_row(f, e), min(run, guests - e)) for f in range(nf) for e in range(0, guests, run)
    ]
    ext_rows = -(-segs * nf * guests // 16) * 16
    direct = slots >= guests and slots % 16 == 0 and half <= 8
    joint_pad = -(-adjacency.shape[1] // 256) * 256
    keys = half_slots + EP
    count = half if direct else 0
    link, link_e, *packed = pl.pallas_call(
        functools.partial(stage_kernel, half_slots, guests, heads, nf, slots, count),
        out_shape=(
            jax.ShapeDtypeStruct((keys, half_slots), F32),
            jax.ShapeDtypeStruct((keys, heads * EQ), F32),
        )
        + (jax.ShapeDtypeStruct((ext_rows, hw), BF),) * count,
        in_specs=[SMEM] + [VMEM] * 4,
        out_specs=(VMEM,) * (2 + count),
        scratch_shapes=[pltpu.VMEM((adjacency.shape[0], joint_pad, joint_pad), F32)],
        compiler_params=pltpu.CompilerParams(vmem_limit_bytes=VMEM_LIMIT),
        name="stage",
    )(flag, send, stream_clip, stream_kind, adjacency)
    if direct:
        ext = lax.ppermute(packed[0], "seq", [(half, 0)])
        for j in range(1, half):
            ext = ext + lax.ppermute(packed[j], "seq", [(half, j)])
    else:
        pieces = [
            recv[a : a + c, s * hw : (s + 1) * hw] for s in range(segs) for a, c in starts
        ]
        pieces.append(jnp.zeros((ext_rows - segs * nf * guests, hw), BF))
        ext = lax.ppermute(
            jnp.concatenate(pieces, axis=0), "seq", [(half + i, i) for i in range(half)]
        )

    main = half_slots
    all_rows = rows + nf * EP
    block_rows = nf * slots
    shared = block_rows % 32 == 0
    out_wide = wide + (LANES if shared else 0)
    head_rows = -(-guests // slots) * block_rows
    head_rows = -(-head_rows // 16) * 16
    pay_rows = -(-(segs * nf * guests + 2 * SUMS) // 8) * 8
    per_frame = (nf, main + EP, hw)
    out, pay, own_sums = pl.pallas_call(
        functools.partial(frame_kernel, half, nf, slots, guests),
        out_shape=(
            jax.ShapeDtypeStruct((rows, out_wide), BF),
            jax.ShapeDtypeStruct((pay_rows, hw), BF),
            jax.ShapeDtypeStruct((8, hw), F32),
        ),
        in_specs=[VMEM, VMEM, SMEM, VMEM, VMEM, SMEM, VMEM, VMEM, VMEM, VMEM, HBM],
        out_specs=(VMEM, VMEM, VMEM),
        scratch_shapes=[
            pltpu.VMEM((all_rows, d), BF),
            pltpu.VMEM((all_rows, d), BF),
            pltpu.VMEM((all_rows, 128), F32),
            pltpu.VMEM((all_rows, 128), F32),
            pltpu.VMEM(per_frame, BF),
            pltpu.VMEM(per_frame, BF),
            pltpu.VMEM(per_frame, BF),
            pltpu.VMEM(per_frame, BF),
            pltpu.VMEM((all_rows, 3 * hw), BF),
            pltpu.VMEM(per_frame, F32),
            pltpu.VMEM(per_frame, F32),
            pltpu.VMEM((all_rows, hw), BF),
            pltpu.VMEM((all_rows, d), F32),
            pltpu.VMEM((d, 3 * hw), BF),
            pltpu.SemaphoreType.DMA((3,)),
        ],
        compiler_params=pltpu.CompilerParams(vmem_limit_bytes=FRAMES_LIMIT),
        name="frames",
    )(
        ext,
        recv,
        flag,
        link,
        link_e,
        graph_coef,
        jnp.repeat(graph_coef, EQ).reshape(1, heads * EQ),
        tok,
        norm_gain.reshape(1, d),
        token_cot,
        w_qkv,
    )

    flip = [(i, (i + half) % n) for i in range(n)]
    got = lax.ppermute(pay, "seq", flip)
    merged, *sums = pl.pallas_call(
        functools.partial(merge_kernel, nf, slots, guests, wide, head_rows),
        out_shape=(
            jax.ShapeDtypeStruct((rows, out_wide), BF),
        )
        + (() if shared else (jax.ShapeDtypeStruct((8, hw), F32),)),
        in_specs=[SMEM] + [VMEM] * 3,
        out_specs=(VMEM,) * (1 if shared else 2),
        input_output_aliases={1: 0},
        compiler_params=pltpu.CompilerParams(vmem_limit_bytes=VMEM_LIMIT),
        name="merge",
    )(flag, out, own_sums, got)
    returned = lax.all_to_all(merged, "seq", 0, 0, axis_index_groups=groups, tiled=True)

    if shared:
        parts = returned.reshape(half, block_rows, out_wide)[:, :32, wide:].astype(F32)
        parts = jnp.sum(parts, axis=0)
        sums = parts[:16] + parts[16:]
    else:
        sums = sums[0]
        k = 1
        while k < half:
            sums = sums + lax.ppermute(sums, "seq", [(i, i ^ k) for i in range(n)])
            k *= 2

    core = lax.ppermute(sums, "dp", [(0, 1), (1, 0)])
    layer_out, grad_x = pl.pallas_call(
        functools.partial(final_kernel, slots, frames),
        out_shape=(
            jax.ShapeDtypeStruct((rows, d), BF),
            jax.ShapeDtypeStruct((rows, d), BF),
        ),
        in_specs=[VMEM, HBM, HBM, VMEM, VMEM, VMEM],
        out_specs=(HBM, HBM),
        scratch_shapes=[
            pltpu.VMEM((rows, d), BF),
            pltpu.VMEM((rows, d), BF),
            pltpu.VMEM((rows, d), BF),
            pltpu.VMEM((rows, d), BF),
            pltpu.SemaphoreType.DMA((6,)),
        ],
        compiler_params=pltpu.CompilerParams(vmem_limit_bytes=VMEM_LIMIT),
        name="final",
    )(returned, x, cot, hid, tok, w_out)
    token, gain, coef = pl.pallas_call(
        sums_kernel,
        out_shape=(
            jax.ShapeDtypeStruct((d,), F32),
            jax.ShapeDtypeStruct((d,), F32),
            jax.ShapeDtypeStruct((1, heads), F32),
        ),
        in_specs=[VMEM, VMEM],
        out_specs=(VMEM, VMEM, VMEM),
        compiler_params=pltpu.CompilerParams(vmem_limit_bytes=VMEM_LIMIT),
        name="sums",
    )(sums, core)

    shape = (1, slots, frames, d)
    return (
        layer_out.reshape(shape),
        grad_x.reshape(shape),
        token,
        gain,
        coef.reshape(-1),
    )


def solution(mesh):
    return jax.shard_map(
        functools.partial(on_device, mesh.shape["seq"]),
        mesh=mesh,
        in_specs=(
            P("dp", "seq", None, None),
            P("dp", "seq", None, None),
            P("dp", "seq", None),
            P("dp", None),
            P("dp", None),
            P(),
            P(),
            P(),
            P(),
            P(),
            P(),
        ),
        out_specs=(P("dp", "seq", None, None), P("dp", "seq", None, None), P(), P(), P()),
        check_vma=False,
    )
```

```python
import functools

import jax
import jax.numpy as jnp
import numpy as np
from jax import lax
from jax.experimental import pallas as pl
from jax.experimental.pallas import tpu as pltpu
from jax.sharding import PartitionSpec as P

BF = jnp.bfloat16
F32 = jnp.float32
BIG_CLIP = 133
HIDDEN_MARK = 64.0
MASKED = -1e30
EP = 16
EQ = 8
VMEM_LIMIT = 16 << 20
FRAMES_LIMIT = 50 << 20
SEND_LIMIT = 56 << 20
SUMS = 5
LANES = 256


def dot_nn(a, b):
    return lax.dot_general(a, b, (((1,), (0,)), ((), ())), preferred_element_type=F32)


def dot_nt(a, b):
    return lax.dot_general(a, b, (((1,), (1,)), ((), ())), preferred_element_type=F32)


def dot_tn(a, b):
    return lax.dot_general(a, b, (((0,), (0,)), ((), ())), preferred_element_type=F32)


def iota(shape, axis):
    return lax.broadcasted_iota(jnp.int32, shape, axis)


def hidden_column(hid, slots, frames, frame_major):
    rows = slots * frames
    r = iota((rows, 1), 0)
    slot_of = r % slots if frame_major else r // frames
    frame_of = r // slots if frame_major else r % frames
    pick_slot = (slot_of == iota((rows, slots), 1)).astype(BF)
    by_slot = dot_nn(pick_slot, hid.astype(F32).astype(BF))
    return jnp.sum(jnp.where(frame_of == iota((rows, frames), 1), by_slot, 0.0), axis=1, keepdims=True)


def row_swap(slots, frames, to_frame_major):
    rows = slots * frames
    r = iota((rows, 1), 0)
    if to_frame_major:
        source = (r % slots) * frames + r // slots
    else:
        source = (r % frames) * slots + r // frames
    return (iota((rows, rows), 1) == source).astype(BF)


def send_kernel(
    slots,
    frames,
    x_hbm,
    cot_hbm,
    hid_hbm,
    w_out_hbm,
    out_ref,
    token_ref,
    x_ref,
    cot_ref,
    hid_ref,
    w_ref,
    sem,
):
    width = x_ref.shape[1]
    copies = [
        pltpu.make_async_copy(hid_hbm, hid_ref, sem.at[0]),
        pltpu.make_async_copy(x_hbm, x_ref, sem.at[1]),
        pltpu.make_async_copy(cot_hbm, cot_ref, sem.at[2]),
        pltpu.make_async_copy(w_out_hbm, w_ref, sem.at[3]),
    ]
    for cp in copies:
        cp.start()
    swap = row_swap(slots, frames, True)
    copies[0].wait()
    hid_t = hidden_column(hid_ref[...], slots, frames, True)
    hid_s = hidden_column(hid_ref[...], slots, frames, False)
    copies[1].wait()
    moved = dot_nn(swap, x_ref[...])
    first = jnp.where(
        (iota((moved.shape[0], 128), 1) == 0) & (hid_t > 0.5), HIDDEN_MARK, moved[:, :128]
    )
    out_ref[:, :128] = first.astype(BF)
    out_ref[:, 128:width] = moved[:, 128:].astype(BF)
    copies[2].wait()
    token_ref[...] = jnp.sum(
        jnp.where(hid_s > 0.5, cot_ref[...].astype(F32), 0.0), axis=0, keepdims=True
    )
    copies[3].wait()
    gc = dot_nt(cot_ref[...], w_ref[...]).astype(BF)
    out_ref[:, width:] = dot_nn(swap, gc).astype(BF)


def final_kernel(
    slots,
    frames,
    recv_ref,
    x_ref,
    cot_ref,
    hid_ref,
    tok_ref,
    w_ref,
    out_hbm,
    grad_hbm,
    out_s,
    grad_s,
    sem,
):
    hw, d = w_ref.shape
    wide = hw + d
    swap = row_swap(slots, frames, False)
    hid = hidden_column(hid_ref[...], slots, frames, False) > 0.5
    ctx = dot_nn(swap, recv_ref[:, :hw]).astype(BF)
    attn = dot_nn(ctx, w_ref[...]).astype(BF)
    delta = dot_nn(swap, recv_ref[:, hw:wide])
    stores = []
    half = swap.shape[0] // 2
    for h in range(2):
        r = slice(h * half, (h + 1) * half)
        here = pl.ds(h * half, half)
        grad_s[r] = jnp.where(hid[r], 0.0, cot_ref[r].astype(F32) + delta[r]).astype(BF)
        stores.append(pltpu.make_async_copy(grad_s.at[here], grad_hbm.at[here], sem.at[2 * h]))
        stores[-1].start()
        x_in = jnp.where(hid[r], tok_ref[...].astype(F32), x_ref[r].astype(F32))
        out_s[r] = (x_in + attn[r].astype(F32)).astype(BF)
        stores.append(pltpu.make_async_copy(out_s.at[here], out_hbm.at[here], sem.at[1 + 2 * h]))
        stores[-1].start()
    for cp in stores:
        cp.wait()


def sums_kernel(here_ref, core_ref, token_ref, gain_ref, coef_ref):
    total = here_ref[...] + core_ref[...]
    width = total.shape[1]
    parts = token_ref.shape[0] // width
    for c in range(parts):
        at = pl.ds(c * width, width)
        token_ref[at] = total[c : c + 1].reshape(width)
        gain_ref[at] = total[parts + c : parts + c + 1].reshape(width)
    coef_ref[...] = total[2 * parts : 2 * parts + 1, : coef_ref.shape[1]]


def split_two(value):
    high = value.astype(BF)
    return high, (value - high.astype(F32)).astype(BF)


def merge_kernel(
    nf, sb, guests, wide, head_rows, flag_ref, buf_ref, own_ref, got_ref, out_ref, *sums_ref
):
    hw = got_ref.shape[1]
    segs = wide // hw
    seg_rows = nf * guests
    total_rows = out_ref.shape[0]
    i = iota((8, got_ref.shape[0]), 0)
    k = iota((8, got_ref.shape[0]), 1) - segs * seg_rows
    pick = ((i < SUMS) & ((k == i) | (k == i + SUMS))).astype(BF)
    sums = own_ref[...] + dot_nn(pick, got_ref[...])
    if sums_ref:
        sums_ref[0][...] = sums
    if out_ref.shape[1] > wide:
        flat = jnp.concatenate(
            [sums[a : a + 1, c : c + LANES] for a in range(SUMS) for c in range(0, hw, LANES)]
            + [jnp.zeros((1, LANES), F32)],
            axis=0,
        )
        block = jnp.concatenate(split_two(flat), axis=0)
        for j in range(total_rows // block.shape[0]):
            out_ref[j * block.shape[0] : (j + 1) * block.shape[0], wide:] = block
    r = iota((head_rows, 1), 0)
    slot = (r // (nf * sb)) * sb + r % sb
    from_row = ((r // sb) % nf) * guests + slot
    guest = jnp.where(slot < guests, 1, 0)
    take = guest * jnp.where(flag_ref[0] == 1, 0, 1)
    for s in range(segs):
        source = jnp.where(guest == 1, s * seg_rows + from_row, 1 << 20)
        pick = (iota((head_rows, got_ref.shape[0]), 1) == source).astype(BF)
        here = slice(s * hw, (s + 1) * hw)
        out_ref[:head_rows, here] = jnp.where(
            take == 1, dot_nn(pick, got_ref[...]), buf_ref[:head_rows, here].astype(F32)
        ).astype(BF)


def local_tables(half_slots, guests, heads, first_half, clip_ref, kind_ref, adj_ref, adj_s):
    total = clip_ref.shape[1]
    kind_count, joint_max = adj_ref.shape[0], adj_ref.shape[1]
    keys = half_slots + EP
    adj_s[...] = jnp.zeros(adj_s.shape, F32)
    adj_s[:, :joint_max, :joint_max] = adj_ref[...].astype(F32)
    i = iota((keys, 1), 0)
    slot = jnp.where(i < half_slots, i + jnp.where(first_half == 1, 0, half_slots), i)
    valid = ((i < half_slots) & (i >= jnp.where(first_half == 1, 0, guests))) | (
        (i >= half_slots) & (i < jnp.where(first_half == 1, half_slots + guests, 0))
    )
    lanes = iota((keys, total), 1)
    at = lanes == slot
    clip_row = clip_ref[...].astype(F32)
    clip = jnp.sum(jnp.where(at, clip_row, 0.0), axis=1, keepdims=True)
    kind = jnp.sum(jnp.where(at, kind_ref[...].astype(F32), 0.0), axis=1, keepdims=True)
    first = jnp.min(
        jnp.where(clip_row == clip, lanes.astype(F32), 1.0 * total), axis=1, keepdims=True
    )
    joint = slot.astype(F32) - first
    clip = jnp.where(valid, clip, -1.0 - i.astype(F32))
    pick = (iota((keys, adj_s.shape[1]), 1).astype(F32) == joint).astype(BF)
    picked = jnp.zeros((keys, adj_s.shape[2]), F32)
    for k in range(kind_count):
        picked = picked + jnp.where(kind == 1.0 * k, dot_nn(pick, adj_s[k].astype(BF)), 0.0)
    link = dot_nt(pick, picked.astype(BF))
    eye = iota((keys, keys), 0) == iota((keys, keys), 1)
    clip_across = jnp.sum(jnp.where(eye, clip, 0.0), axis=0, keepdims=True)
    link = jnp.where(clip == clip_across, link, -1.0)
    tile = (iota((EP, heads * EQ), 1) % EQ == iota((EP, heads * EQ), 0)).astype(BF)
    return link[:, :half_slots], dot_nn(link[:, half_slots:].astype(BF), tile)


def stage_kernel(
    half_slots, guests, heads, nf, sb, count, flag_ref, send_ref, clip_ref, kind_ref, adj_ref, *refs
):
    link_ref, link_e_ref = refs[:2]
    ext_refs = refs[2 : 2 + count]
    adj_s = refs[-1]

    @pl.when(flag_ref[1] == count)
    def _():
        for j, ref in enumerate(ext_refs):
            ext_rows, hw = ref.shape
            pieces = [
                send_ref[(j * nf + f) * sb : (j * nf + f + 1) * sb, c : c + hw].astype(F32)[:guests]
                for c in range(0, send_ref.shape[1], hw)
                for f in range(nf)
            ]
            pieces.append(jnp.zeros((ext_rows - len(pieces) * guests, hw), F32))
            ref[...] = jnp.concatenate(pieces, axis=0).astype(BF)

    link, link_e = local_tables(
        half_slots, guests, heads, flag_ref[0], clip_ref, kind_ref, adj_ref, adj_s
    )
    link_ref[...] = link
    link_e_ref[...] = link_e


def frame_kernel(
    blocks,
    nf,
    sb,
    guests,
    *refs,
):
    (
        ext_ref,
        recv_ref,
        flag_ref,
        link_ref,
        link_e_ref,
        coef_ref,
        coef_e_ref,
        tok_ref,
        gain_ref,
        token_in_ref,
        w_hbm,
        out_s,
        pay_ref,
        sums_ref,
        x_s,
        xn_s,
        inv_s,
        hid_s,
        q_s,
        k_s,
        v_s,
        g_s,
        gu_s,
        gk_s,
        gv_s,
        ctx_s,
        gn_s,
        w_ref,
        sem,
    ) = refs
    d = gain_ref.shape[1]
    hw = w_ref.shape[1] // 3
    main = blocks * sb
    keys = main + EP
    rows = nf * main
    all_rows = rows + nf * EP
    heads = coef_ref.shape[0]
    hs = hw // heads
    seg_rows = nf * guests
    aligned = sb % 16 == 0

    copies = [pltpu.make_async_copy(w_hbm, w_ref, sem.at[0])]
    for cp in copies:
        cp.start()
    link = link_ref[...]
    link_e = link_e_ref[...]

    def gather(value):
        if aligned:
            return jnp.concatenate(
                [
                    value[(j * nf + f) * sb : (j * nf + f + 1) * sb]
                    for f in range(nf)
                    for j in range(blocks)
                ],
                axis=0,
            )
        r = iota((rows, 1), 0)
        slot = r % main
        source = ((slot // sb) * nf + r // main) * sb + slot % sb
        return dot_nn((iota((rows, rows), 1) == source).astype(BF), value).astype(BF)

    def scatter(value):
        if aligned:
            return jnp.concatenate(
                [
                    value[f * main + j * sb : f * main + (j + 1) * sb]
                    for j in range(blocks)
                    for f in range(nf)
                ],
                axis=0,
            )
        r = iota((rows, 1), 0)
        pair = r // sb
        source = (pair % nf) * main + (pair // nf) * sb + r % sb
        return dot_nn((iota((rows, rows), 1) == source).astype(BF), value).astype(BF)

    er = iota((nf * EP, 1), 0)
    guest_row = jnp.where(er % EP < guests, (er // EP) * guests + er % EP, 1 << 20)

    def guest_segment(seg):
        pick = (iota((nf * EP, ext_ref.shape[0]), 1) == guest_row + seg * seg_rows).astype(BF)
        return dot_nn(pick, ext_ref[...]).astype(BF)

    for c in range(d // hw):
        x_s[rows:, c * hw : (c + 1) * hw] = guest_segment(c)
    x_s[:rows] = gather(recv_ref[:, :d])
    tok = tok_ref[...]
    gain = gain_ref[...]
    for a in range(0, all_rows, 16):
        xb = x_s[a : a + 16]
        hid = xb[:, 0:1].astype(F32) > 0.5 * HIDDEN_MARK
        xf = jnp.where(hid, tok.astype(F32), xb.astype(F32))
        x_s[a : a + 16] = xf.astype(BF)
        inv = 1.0 / jnp.sqrt(jnp.mean(xf * xf, axis=1, keepdims=True) + 1e-6)
        inv_s[a : a + 16] = jnp.broadcast_to(inv, (16, 128))
        hid_s[a : a + 16] = jnp.broadcast_to(jnp.where(hid, 1.0, 0.0), (16, 128))
        xn_s[a : a + 16] = (xf * inv * gain).astype(BF)

    for cp in copies:
        cp.wait()
    for c, ref in enumerate((q_s, k_s, v_s)):
        part = dot_nn(xn_s[...], w_ref[:, c * hw : (c + 1) * hw]).astype(BF)
        if c == 0:
            part = part * BF(hs**-0.5)
        for f in range(nf):
            ref[f, :main] = part[f * main : (f + 1) * main]
            ref[f, main:] = part[rows + f * EP : rows + (f + 1) * EP]

    gc_main = gather(recv_ref[:, d:])
    gc_ext = guest_segment(d // hw)
    for f in range(nf):
        g_s[f, :main] = gc_main[f * main : (f + 1) * main]
        g_s[f, main:] = gc_ext[f * EP : (f + 1) * EP]

    own = (iota((heads * EQ, hw), 0) // EQ == iota((heads * EQ, hw), 1) // hs)
    bias_e = jnp.where(link_e < 0, MASKED, coef_e_ref[...] * link_e)
    coef_lanes = jnp.zeros((1, heads * EQ), F32)

    def spread(value):
        tall = jnp.concatenate([value] * heads, axis=0)
        return jnp.where(own, tall, jnp.zeros_like(tall))

    def fold(value):
        kept = jnp.where(own, value, 0.0)
        total = kept[0:EQ]
        for h in range(1, heads):
            total = total + kept[h * EQ : (h + 1) * EQ]
        return jnp.concatenate([total, jnp.zeros((EP - EQ, hw), F32)], axis=0)

    def attend(scores, grad_w):
        n = range(len(scores))
        top = [jnp.max(scores[i], axis=0, keepdims=True) for i in n]
        raw = [jnp.exp(scores[i] - top[i]) for i in n]
        w_t = [raw[i] * (1.0 / jnp.sum(raw[i], axis=0, keepdims=True)) for i in n]
        w_b = [w_t[i].astype(BF) for i in n]
        ds = [
            w_t[i] * (grad_w[i] - jnp.sum(w_t[i] * grad_w[i], axis=0, keepdims=True)) for i in n
        ]
        return w_t, w_b, ds, [ds[i].astype(BF) for i in n]

    fs = range(nf)
    q_e = [spread(q_s[f, main:].astype(F32)[:EQ]).astype(BF) for f in fs]
    g_e = [spread(g_s[f, main:].astype(F32)[:EQ]).astype(BF) for f in fs]
    s_t = [dot_nt(k_s[f], q_e[f]) + bias_e for f in fs]
    gw = [dot_nt(v_s[f], g_e[f]) for f in fs]
    w_t, w_b, ds, ds_b = attend(s_t, gw)
    for f in fs:
        coef_lanes = coef_lanes + jnp.sum(ds[f] * link_e, axis=0, keepdims=True)
    ctx_e = [dot_tn(w_b[f], v_s[f]) for f in fs]
    gq_e = [dot_tn(ds_b[f], k_s[f]) for f in fs]
    for f in fs:
        guest_rows = slice(rows + f * EP, rows + (f + 1) * EP)
        gk_s[f] = dot_nn(ds_b[f], q_e[f])
        gv_s[f] = dot_nn(w_b[f], g_e[f])
        ctx_s[guest_rows] = fold(ctx_e[f]).astype(BF)
        gu_s[guest_rows, :hw] = fold(gq_e[f] * hs**-0.5).astype(BF)

    lane = iota((1, 128), 1)
    coef_out = jnp.zeros((1, 128), F32)
    for h in range(heads):
        coef_out = coef_out + jnp.where(
            lane == h, jnp.sum(coef_lanes[:, h * EQ : (h + 1) * EQ]), 0.0
        )

    pair_w = 2 * hs
    low = iota((main, pair_w), 1) < hs
    zero = jnp.zeros((main, pair_w), BF)
    link_two = jnp.concatenate([link, link], axis=1)

    def two_heads(value):
        return jnp.concatenate(
            [jnp.where(low, value, zero), jnp.where(low, zero, value)], axis=0
        )

    for first_pair in range(0, heads // 2, 3):
        pairs = range(first_pair, min(first_pair + 3, heads // 2))
        items = [(p, f) for p in pairs for f in range(nf)]
        bias = {
            p: jnp.concatenate(
                [
                    jnp.where(link < 0, MASKED, coef_ref[2 * p] * link),
                    jnp.where(link < 0, MASKED, coef_ref[2 * p + 1] * link),
                ],
                axis=1,
            )
            for p in pairs
        }
        cols = {p: slice(p * pair_w, (p + 1) * pair_w) for p in pairs}
        k = [k_s[f, :, cols[p]] for p, f in items]
        v = [v_s[f, :, cols[p]] for p, f in items]
        qq = [two_heads(q_s[f, :main, cols[p]]) for p, f in items]
        gg = [two_heads(g_s[f, :main, cols[p]]) for p, f in items]
        s_t = [dot_nt(k[i], qq[i]) + bias[p] for i, (p, f) in enumerate(items)]
        gw = [dot_nt(v[i], gg[i]) for i in range(len(items))]
        w_t, w_b, ds, ds_b = attend(s_t, gw)
        ctx_t = [dot_tn(v[i], w_b[i]) for i in range(len(items))]
        gv = [gv_s[f, :, cols[p]] + dot_nn(w_b[i], gg[i]) for i, (p, f) in enumerate(items)]
        gq_t = [dot_tn(k[i], ds_b[i]) for i in range(len(items))]
        gk = [gk_s[f, :, cols[p]] + dot_nn(ds_b[i], qq[i]) for i, (p, f) in enumerate(items)]
        for i, (p, f) in enumerate(items):
            main_rows = slice(f * main, (f + 1) * main)
            guest_rows = slice(rows + f * EP, rows + (f + 1) * EP)
            both = jnp.concatenate([ctx_t[i][:hs, :main], ctx_t[i][hs:, main:]], axis=0)
            ctx_s[main_rows, cols[p]] = both.T.astype(BF)
            both = jnp.concatenate([gq_t[i][:hs, :main], gq_t[i][hs:, main:]], axis=0)
            gu_s[main_rows, cols[p]] = (both.T * hs**-0.5).astype(BF)
            for value, offset in ((gk[i].astype(BF), hw), (gv[i].astype(BF), 2 * hw)):
                here = slice(offset + p * pair_w, offset + (p + 1) * pair_w)
                gu_s[main_rows, here] = value[:main]
                gu_s[guest_rows, here] = value[main:]
        for p in pairs:
            ds_sum = functools.reduce(
                lambda x, y: x + y, [ds[i] for i, item in enumerate(items) if item[0] == p]
            )
            lanes = jnp.sum(ds_sum * link_two, axis=0, keepdims=True)
            coef_out = coef_out + jnp.where(lane == 2 * p, jnp.sum(lanes[:, :main]), 0.0)
            coef_out = coef_out + jnp.where(lane == 2 * p + 1, jnp.sum(lanes[:, main:]), 0.0)

    out_s[:, :hw] = scatter(ctx_s[:rows])

    gn_s[...] = dot_nt(gu_s[...], w_ref[...])
    guest_limit = jnp.where(flag_ref[0] == 1, guests, 0)
    main_limit = jnp.where(flag_ref[0] == 1, 0, guests)
    place = iota((16, 1), 0)
    token_sum = jnp.zeros((8, d), F32)
    gain_sum = jnp.zeros((8, d), F32)
    for a in range(0, all_rows, 16):
        gn = gn_s[a : a + 16]
        inv = inv_s[a : a + 16, 0:1]
        x_unit = x_s[a : a + 16].astype(F32) * inv
        g_gain = gn * gain
        gx = gn * x_unit
        mean_gx = jnp.mean(gx * gain, axis=1, keepdims=True)
        delta = (g_gain - x_unit * mean_gx) * inv
        if a >= rows:
            x_s[a : a + 16] = delta.astype(BF)
            valid = jnp.where(place < guest_limit, 1.0, 0.0)
        elif aligned:
            f, j = a // main, (a % main) // sb
            at = (j * nf + f) * sb + a % sb
            out_s[at : at + 16, hw : hw + d] = delta.astype(BF)
            valid = jnp.where(place + a % main >= main_limit, 1.0, 0.0)
        else:
            x_s[a : a + 16] = delta.astype(BF)
            valid = jnp.where(place + a % main >= main_limit, 1.0, 0.0)
        hid_valid = hid_s[a : a + 16, 0:1] * valid
        if a >= rows or a % main < guests:
            gx = gx * valid
        delta = delta * hid_valid
        gain_sum = gain_sum + (gx[:8] + gx[8:])
        token_sum = token_sum + (delta[:8] + delta[8:])
    if not aligned:
        out_s[:, hw : hw + d] = scatter(x_s[:rows])
    gain_sum = jnp.sum(gain_sum, axis=0, keepdims=True)
    token_sum = token_in_ref[...] + jnp.sum(token_sum, axis=0, keepdims=True)
    coef_row = jnp.concatenate([coef_out, jnp.zeros((1, hw - coef_out.shape[1]), F32)], axis=1)
    sums = jnp.concatenate(
        [token_sum[:, :hw], token_sum[:, hw:], gain_sum[:, :hw], gain_sum[:, hw:], coef_row]
        + [jnp.zeros((8 - SUMS, hw), F32)],
        axis=0,
    )
    high, low_part = split_two(sums)
    sums_ref[...] = high.astype(F32) + low_part.astype(F32)
    pair = jnp.concatenate([high.astype(F32), low_part.astype(F32)], axis=0).astype(BF)
    orow = iota((pay_ref.shape[0], 1), 0)
    k = orow - (1 + d // hw) * seg_rows
    source = jnp.where(
        k < 0, 1 << 20, jnp.where(k < SUMS, k, jnp.where(k < 2 * SUMS, k - SUMS + 8, 1 << 20))
    )
    total = dot_nn((iota((pay_ref.shape[0], 16), 1) == source).astype(BF), pair)
    inner = orow % seg_rows
    for s in range(1 + d // hw):
        piece = ctx_s[rows:] if s == 0 else x_s[rows:, (s - 1) * hw : s * hw]
        source = jnp.where(
            orow // seg_rows == s, (inner // guests) * EP + inner % guests, 1 << 20
        )
        total = total + dot_nn(
            (iota((pay_ref.shape[0], nf * EP), 1) == source).astype(BF), piece
        )
    pay_ref[...] = total.astype(BF)


VMEM = pl.BlockSpec(memory_space=pltpu.VMEM)
SMEM = pl.BlockSpec(memory_space=pltpu.SMEM)
HBM = pl.BlockSpec(memory_space=pl.ANY)


def on_device(
    n,
    joints_x,
    cotangent,
    hidden,
    stream_clip,
    stream_kind,
    adjacency,
    mask_token,
    norm_gain,
    w_qkv,
    w_out,
    graph_coef,
):
    _, slots, frames, d = joints_x.shape
    hw = w_out.shape[0]
    heads = graph_coef.shape[0]
    total = stream_clip.shape[1]
    half = n // 2
    nf = frames // half
    half_slots = total // 2
    guests = BIG_CLIP - half_slots
    rows = slots * frames
    wide = d + hw
    segs = wide // hw
    me = lax.axis_index("seq")
    first_half = me < half
    groups = [list(range(half)), list(range(half, n))]

    x = joints_x.reshape(rows, d)
    cot = cotangent.reshape(rows, d)
    hid = hidden[0]
    tok = mask_token.reshape(1, d)
    flag = jnp.stack([first_half.astype(jnp.int32), me])

    send, token_cot = pl.pallas_call(
        functools.partial(send_kernel, slots, frames),
        out_shape=(
            jax.ShapeDtypeStruct((rows, wide), BF),
            jax.ShapeDtypeStruct((1, d), F32),
        ),
        in_specs=[HBM] * 4,
        out_specs=(VMEM, VMEM),
        scratch_shapes=[
            pltpu.VMEM((rows, d), BF),
            pltpu.VMEM((rows, d), BF),
            pltpu.VMEM(hid.shape, jnp.int32),
            pltpu.VMEM(w_out.shape, BF),
            pltpu.SemaphoreType.DMA((4,)),
        ],
        compiler_params=pltpu.CompilerParams(vmem_limit_bytes=SEND_LIMIT),
        name="send",
    )(x, cot, hid, w_out)

    recv = lax.all_to_all(send, "seq", 0, 0, axis_index_groups=groups, tiled=True)

    def buffer_row(f, e):
        return ((e // slots) * nf + f) * slots + e % slots

    run = min(slots, guests)
    starts = [
        (buffer_row(f, e), min(run, guests - e)) for f in range(nf) for e in range(0, guests, run)
    ]
    ext_rows = -(-segs * nf * guests // 16) * 16
    direct = slots >= guests and slots % 16 == 0 and half <= 8
    joint_pad = -(-adjacency.shape[1] // 256) * 256
    keys = half_slots + EP
    count = half if direct else 0
    link, link_e, *packed = pl.pallas_call(
        functools.partial(stage_kernel, half_slots, guests, heads, nf, slots, count),
        out_shape=(
            jax.ShapeDtypeStruct((keys, half_slots), F32),
            jax.ShapeDtypeStruct((keys, heads * EQ), F32),
        )
        + (jax.ShapeDtypeStruct((ext_rows, hw), BF),) * count,
        in_specs=[SMEM] + [VMEM] * 4,
        out_specs=(VMEM,) * (2 + count),
        scratch_shapes=[pltpu.VMEM((adjacency.shape[0], joint_pad, joint_pad), F32)],
        compiler_params=pltpu.CompilerParams(vmem_limit_bytes=VMEM_LIMIT),
        name="stage",
    )(flag, send, stream_clip, stream_kind, adjacency)
    if direct:
        ext = lax.ppermute(packed[0], "seq", [(half, 0)])
        for j in range(1, half):
            ext = ext + lax.ppermute(packed[j], "seq", [(half, j)])
    else:
        pieces = [
            recv[a : a + c, s * hw : (s + 1) * hw] for s in range(segs) for a, c in starts
        ]
        pieces.append(jnp.zeros((ext_rows - segs * nf * guests, hw), BF))
        ext = lax.ppermute(
            jnp.concatenate(pieces, axis=0), "seq", [(half + i, i) for i in range(half)]
        )

    main = half_slots
    all_rows = rows + nf * EP
    block_rows = nf * slots
    shared = block_rows % 32 == 0
    out_wide = wide + (LANES if shared else 0)
    head_rows = -(-guests // slots) * block_rows
    head_rows = -(-head_rows // 16) * 16
    pay_rows = -(-(segs * nf * guests + 2 * SUMS) // 8) * 8
    per_frame = (nf, main + EP, hw)
    out, pay, own_sums = pl.pallas_call(
        functools.partial(frame_kernel, half, nf, slots, guests),
        out_shape=(
            jax.ShapeDtypeStruct((rows, out_wide), BF),
            jax.ShapeDtypeStruct((pay_rows, hw), BF),
            jax.ShapeDtypeStruct((8, hw), F32),
        ),
        in_specs=[VMEM, VMEM, SMEM, VMEM, VMEM, SMEM, VMEM, VMEM, VMEM, VMEM, HBM],
        out_specs=(VMEM, VMEM, VMEM),
        scratch_shapes=[
            pltpu.VMEM((all_rows, d), BF),
            pltpu.VMEM((all_rows, d), BF),
            pltpu.VMEM((all_rows, 128), F32),
            pltpu.VMEM((all_rows, 128), F32),
            pltpu.VMEM(per_frame, BF),
            pltpu.VMEM(per_frame, BF),
            pltpu.VMEM(per_frame, BF),
            pltpu.VMEM(per_frame, BF),
            pltpu.VMEM((all_rows, 3 * hw), BF),
            pltpu.VMEM(per_frame, F32),
            pltpu.VMEM(per_frame, F32),
            pltpu.VMEM((all_rows, hw), BF),
            pltpu.VMEM((all_rows, d), F32),
            pltpu.VMEM((d, 3 * hw), BF),
            pltpu.SemaphoreType.DMA((3,)),
        ],
        compiler_params=pltpu.CompilerParams(vmem_limit_bytes=FRAMES_LIMIT),
        name="frames",
    )(
        ext,
        recv,
        flag,
        link,
        link_e,
        graph_coef,
        jnp.repeat(graph_coef, EQ).reshape(1, heads * EQ),
        tok,
        norm_gain.reshape(1, d),
        token_cot,
        w_qkv,
    )

    flip = [(i, (i + half) % n) for i in range(n)]
    got = lax.ppermute(pay, "seq", flip)
    merged, *sums = pl.pallas_call(
        functools.partial(merge_kernel, nf, slots, guests, wide, head_rows),
        out_shape=(
            jax.ShapeDtypeStruct((rows, out_wide), BF),
        )
        + (() if shared else (jax.ShapeDtypeStruct((8, hw), F32),)),
        in_specs=[SMEM] + [VMEM] * 3,
        out_specs=(VMEM,) * (1 if shared else 2),
        input_output_aliases={1: 0},
        compiler_params=pltpu.CompilerParams(vmem_limit_bytes=VMEM_LIMIT),
        name="merge",
    )(flag, out, own_sums, got)
    returned = lax.all_to_all(merged, "seq", 0, 0, axis_index_groups=groups, tiled=True)

    if shared:
        parts = returned.reshape(half, block_rows, out_wide)[:, :32, wide:].astype(F32)
        parts = jnp.sum(parts, axis=0)
        sums = parts[:16] + parts[16:]
    else:
        sums = sums[0]
        k = 1
        while k < half:
            sums = sums + lax.ppermute(sums, "seq", [(i, i ^ k) for i in range(n)])
            k *= 2

    core = lax.ppermute(sums, "dp", [(0, 1), (1, 0)])
    layer_out, grad_x = pl.pallas_call(
        functools.partial(final_kernel, slots, frames),
        out_shape=(
            jax.ShapeDtypeStruct((rows, d), BF),
            jax.ShapeDtypeStruct((rows, d), BF),
        ),
        in_specs=[VMEM] * 6,
        out_specs=(HBM, HBM),
        scratch_shapes=[
            pltpu.VMEM((rows, d), BF),
            pltpu.VMEM((rows, d), BF),
            pltpu.SemaphoreType.DMA((4,)),
        ],
        compiler_params=pltpu.CompilerParams(vmem_limit_bytes=VMEM_LIMIT),
        name="final",
    )(returned, x, cot, hid, tok, w_out)
    token, gain, coef = pl.pallas_call(
        sums_kernel,
        out_shape=(
            jax.ShapeDtypeStruct((d,), F32),
            jax.ShapeDtypeStruct((d,), F32),
            jax.ShapeDtypeStruct((1, heads), F32),
        ),
        in_specs=[VMEM, VMEM],
        out_specs=(VMEM, VMEM, VMEM),
        compiler_params=pltpu.CompilerParams(vmem_limit_bytes=VMEM_LIMIT),
        name="sums",
    )(sums, core)

    shape = (1, slots, frames, d)
    return (
        layer_out.reshape(shape),
        grad_x.reshape(shape),
        token,
        gain,
        coef.reshape(-1),
    )


def solution(mesh):
    return jax.shard_map(
        functools.partial(on_device, mesh.shape["seq"]),
        mesh=mesh,
        in_specs=(
            P("dp", "seq", None, None),
            P("dp", "seq", None, None),
            P("dp", "seq", None),
            P("dp", None),
            P("dp", None),
            P(),
            P(),
            P(),
            P(),
            P(),
            P(),
        ),
        out_specs=(P("dp", "seq", None, None), P("dp", "seq", None, None), P(), P(), P()),
        check_vma=False,
    )
```
